32 devices in a mesh: groups: 2 (over y), dp: 16 (over z, x, core).
Axes of the slice: x: 2, y: 2, z: 4, core: 2. Of those that a mesh axis runs over, the one named last changes fastest.
Arguments:
- node_feats: bfloat16 [4096, 3712], P(('groups', 'dp')), parts along dimension 0, may hold values from -6 to 6
- node_grad: bfloat16 [4096, 3712], P(('groups', 'dp')), parts along dimension 0, may hold values from -6 to 6
- flat_params: bfloat16 [21888, 128], P('dp'), may hold values from -0.21875 to 0.21875
- rot_table: bfloat16 [64, 29, 29], replicated, may hold values from -0.41 to 1.41
- edge_src: int32 [4096], P(('groups', 'dp')), parts along dimension 0, may hold values from 0 to 127
- edge_dst: int32 [4096], P(('groups', 'dp')), parts along dimension 0, may hold values from 0 to 127
- edge_rot: int32 [4096], P(('groups', 'dp')), parts along dimension 0, may hold values from 0 to 63
- edge_owner: int32 [4096, 1], P(('groups', 'dp')), parts along dimension 0, may hold values from 0 to 15, as said below
Outputs:
- node_out: bfloat16 [4096, 3712], P(('groups', 'dp')), parts along dimension 0
- weight_grad: float32 [43776, 128], P(('groups', 'dp')), parts along dimension 0
The draws below stay inside these ranges and needn't reach their ends.
There are 2 independent parts, one for each index of `groups`. The reference program is written for one: setup_inputs(seed, part) draws one part's arguments, and reference() takes and returns one part's arrays. A program takes and returns all parts, laid end to end along the dimension named above; an argument that names none is the same for every part. Nothing has to cross between parts.
Inputs may be any that keep to these rules, and one draw needn't show every extreme that they name: `edge_owner`: dp indices form aligned runs of 8; an edge's owner lies in the run of the edge's own device, at most two indices away from it; exactly half of each device's 128 edges are owned by the device itself, and no other owner is named by more than 32 of them.
All inputs are finite; a program needn't handle non-finite values.
Results may differ from the reference program's by a relative error of at most 0.0058.
Values may be sent and summed in bfloat16 or wider, within the bound.
No kernel may reach another device: no remote copies, remote signals or barrier semaphores. Data moves between devices by JAX's collectives and lax.ppermute only.
A program may use at most 128 MiB of HBM per device.

```python
import math
import jax
import jax.numpy as jnp
from jax import lax

C = 128
K = 29
NROT = 64
SPAN = 8
NODE_DEV = 128
E_DEV = 128
NODES = 2048
EDGES = 2048
CAP = 32
PROWS = 21888
N_DP = 16


def draw_rot_table(key, part):
    key = jax.random.fold_in(key, 11)
    noise = jnp.clip(jax.random.normal(key, (NROT, K, K), jnp.float32), -4.0, 4.0) * 0.1
    return (jnp.eye(K, dtype=jnp.float32)[None, :, :] + noise).astype(jnp.bfloat16)


def draw_edge_owner(key, part):
    key = jax.random.fold_in(key, 23)
    first_key, second_key, third_key = jax.random.split(key, 3)
    devices = jnp.arange(N_DP, dtype=jnp.int32)
    position = devices % SPAN
    reach = jnp.array([-2, -1, 1, 2], jnp.int32)
    landing = position[:, None] + reach[None, :]
    valid = (landing >= 0) & (landing < SPAN)
    columns = jnp.arange(4, dtype=jnp.int32)
    main_scores = jax.random.randint(first_key, (N_DP, 4), 0, 1 << 20, jnp.int32) * 4 + columns[None, :]
    main_scores = jnp.where(valid, main_scores, -1)
    main_pick = lax.top_k(main_scores, 1)[1][:, 0]
    other_scores = jax.random.randint(second_key, (N_DP, CAP, 4), 0, 1 << 20, jnp.int32) * 4 + columns[None, None, :]
    allowed = valid[:, None, :] & (columns[None, None, :] != main_pick[:, None, None])
    other_scores = jnp.where(allowed, other_scores, -1)
    other_pick = lax.top_k(other_scores, 1)[1][:, :, 0]
    local_part = jnp.zeros((N_DP, E_DEV - 2 * CAP), jnp.int32)
    main_part = jnp.broadcast_to(reach[main_pick][:, None], (N_DP, CAP))
    other_part = reach[other_pick]
    offsets = jnp.concatenate([local_part, main_part, other_part], axis=1)
    order_scores = jax.random.randint(third_key, (N_DP, E_DEV), 0, 1 << 20, jnp.int32) * E_DEV + jnp.arange(E_DEV, dtype=jnp.int32)[None, :]
    order = jnp.argsort(order_scores, axis=1)
    offsets = jnp.take_along_axis(offsets, order, axis=1)
    owners = devices[:, None] + offsets
    return owners.reshape(EDGES, 1).astype(jnp.int32)


def touch_ends(entries, own_key, smallest, high):
    longest = entries.shape.index(max(entries.shape))
    spots = []
    for shift in (0, 1):
        where = [jax.random.randint(jax.random.fold_in(own_key, axis), (), 0, length) for axis, length in enumerate(entries.shape)]
        where[longest] = (where[longest] + shift) % entries.shape[longest]
        spots.append(tuple(where))
    return entries.at[spots[0]].set(smallest).at[spots[1]].set(high)


def block_levels(own_key, shape, shards, smallest, largest):
    level = 1.0
    for dim, parts in shards:
        draws = jax.random.uniform(jax.random.fold_in(jax.random.fold_in(own_key, 6), dim), (parts,), jnp.float32, smallest / len(shards), largest / len(shards))
        level = level * jnp.repeat(jnp.exp(draws), shape[dim] // parts).reshape((-1,) + (1,) * (len(shape) - 1 - dim))
    return level


def centred(key, dims, width, limit, cuts=(), kind=jnp.bfloat16):
    drawn = jax.random.normal(key, dims, jnp.float32) * width
    if len(cuts) > 0:
        drawn = block_levels(key, dims, cuts, -0.22, 0.18) * drawn
    return jnp.clip(drawn, min=-limit, max=limit).astype(kind)


def setup_inputs(seed: int = 0, part: int = 0) -> dict:
    key_of = jax.random.split(jax.random.key(seed), 9)
    own_keys = jax.random.split(jax.random.fold_in(key_of[8], part), 9)
    return {
        "node_feats": centred(own_keys[0], (NODES, K * C), 1.0, 6.0, ((0, 16),)),
        "node_grad": centred(own_keys[1], (NODES, K * C), 1.0, 6.0, ((0, 16),)),
        "flat_params": centred(key_of[2], (PROWS, 128), (6 * C) ** -0.5, 0.21875, ((0, 16),)),
        "rot_table": draw_rot_table(jax.random.fold_in(key_of[8], 71), part),
        "edge_src": touch_ends(jax.random.randint(own_keys[4], (EDGES,), 0, NODE_DEV), jax.random.fold_in(own_keys[4], 1), 0, NODE_DEV - 1).astype(jnp.int32),
        "edge_dst": touch_ends(jax.random.randint(own_keys[5], (EDGES,), 0, NODE_DEV), jax.random.fold_in(own_keys[5], 1), 0, NODE_DEV - 1).astype(jnp.int32),
        "edge_rot": touch_ends(jax.random.randint(own_keys[6], (EDGES,), 0, NROT), jax.random.fold_in(own_keys[6], 1), 0, NROT - 1).astype(jnp.int32),
        "edge_owner": draw_edge_owner(jax.random.fold_in(jax.random.fold_in(key_of[8], part), 71), part),
    }


def unpack(flat_vector, channels):
    first_size = 49 * channels * channels
    second_size = 36 * channels * channels
    third_size = 25 * channels * channels
    offset = 0
    first = flat_vector[offset:offset + first_size].reshape(7 * channels, 7 * channels)
    offset = offset + first_size
    one_real = flat_vector[offset:offset + second_size].reshape(6 * channels, 6 * channels)
    offset = offset + second_size
    one_imag = flat_vector[offset:offset + second_size].reshape(6 * channels, 6 * channels)
    offset = offset + second_size
    two_real = flat_vector[offset:offset + third_size].reshape(5 * channels, 5 * channels)
    offset = offset + third_size
    two_imag = flat_vector[offset:offset + third_size].reshape(5 * channels, 5 * channels)
    return (first, one_real, one_imag, two_real, two_imag)

def blocks_of(rows, channels):
    edges_at = [0, 7, 13, 19, 24, 29]
    return [rows[:, edges_at[i] * channels:edges_at[i + 1] * channels] for i in range(5)]

def multiply(left, right):
    return jnp.dot(left, right, preferred_element_type=jnp.float32)

def convolve(rotated, weights, channels):
    first, one_real, one_imag, two_real, two_imag = weights
    zero_part, real_one, imag_one, real_two, imag_two = blocks_of(rotated, channels)
    out_zero = multiply(zero_part, first)
    out_real1 = multiply(real_one, one_real) - multiply(imag_one, one_imag)
    out_imag1 = multiply(real_one, one_imag) + multiply(imag_one, one_real)
    out_real2 = multiply(real_two, two_real) - multiply(imag_two, two_imag)
    out_imag2 = multiply(real_two, two_imag) + multiply(imag_two, two_real)
    joined = jnp.concatenate([out_zero, out_real1, out_imag1, out_real2, out_imag2], axis=1)
    return joined.astype(jnp.bfloat16)

def outer_sum(left, right):
    return lax.dot_general(left, right, (((0,), (0,)), ((), ())), preferred_element_type=jnp.float32)

def weight_terms(rotated, upstream, channels):
    zero_part, real_one, imag_one, real_two, imag_two = blocks_of(rotated, channels)
    up_zero, up_real1, up_imag1, up_real2, up_imag2 = blocks_of(upstream, channels)
    grad_first = outer_sum(zero_part, up_zero)
    grad_real1 = outer_sum(real_one, up_real1) + outer_sum(imag_one, up_imag1)
    grad_imag1 = outer_sum(real_one, up_imag1) - outer_sum(imag_one, up_real1)
    grad_real2 = outer_sum(real_two, up_real2) + outer_sum(imag_two, up_imag2)
    grad_imag2 = outer_sum(real_two, up_imag2) - outer_sum(imag_two, up_real2)
    return jnp.concatenate([grad_first.reshape(-1), grad_real1.reshape(-1), grad_imag1.reshape(-1), grad_real2.reshape(-1), grad_imag2.reshape(-1)])

def reference(node_feats, node_grad, flat_params, rot_table, edge_src, edge_dst, edge_rot, edge_owner):
    weights = unpack(flat_params.reshape(-1), C)
    table = rot_table.astype(jnp.float32)
    owners = edge_owner[:, 0]

    def scan_step(state_pair, block_index):
        totals, grad_sum = state_pair
        start = block_index * E_DEV
        sources = lax.dynamic_slice_in_dim(edge_src, start, E_DEV) + block_index * NODE_DEV
        targets = lax.dynamic_slice_in_dim(owners, start, E_DEV) * NODE_DEV + lax.dynamic_slice_in_dim(edge_dst, start, E_DEV)
        turn_ids = lax.dynamic_slice_in_dim(edge_rot, start, E_DEV)
        matrices = table[turn_ids]
        features = node_feats[sources].reshape(E_DEV, K, C).astype(jnp.float32)
        rotated = jnp.einsum('ekj,ejc->ekc', matrices, features, precision=lax.Precision.HIGHEST)
        rotated = rotated.astype(jnp.bfloat16).reshape(E_DEV, K * C)
        message = convolve(rotated, weights, C)
        spread = jnp.einsum('ejk,ejc->ekc', matrices, message.reshape(E_DEV, K, C).astype(jnp.float32), precision=lax.Precision.HIGHEST)
        totals = totals.at[targets].add(spread.reshape(E_DEV, K * C))
        incoming = node_grad[targets].reshape(E_DEV, K, C).astype(jnp.float32)
        upstream = jnp.einsum('ekj,ejc->ekc', matrices, incoming, precision=lax.Precision.HIGHEST)
        upstream = upstream.astype(jnp.bfloat16).reshape(E_DEV, K * C)
        grad_sum = grad_sum + weight_terms(rotated, upstream, C)
        return ((totals, grad_sum), None)
    start_pair = (jnp.zeros((NODES, K * C), jnp.float32), jnp.zeros((171 * C * C,), jnp.float32))
    (totals, grad_sum), _ = lax.scan(scan_step, start_pair, jnp.arange(N_DP, dtype=jnp.int32))
    node_out = totals.astype(jnp.bfloat16)
    scaled = grad_sum * (1.0 / math.sqrt(EDGES))
    padded = jnp.concatenate([scaled, jnp.zeros((PROWS * 128 - 171 * C * C,), jnp.float32)])
    return (node_out, padded.reshape(PROWS, 128))
```

```python
import math

import jax
import jax.numpy as jnp
import numpy as np
from jax import lax
from jax.experimental import pallas as pl
from jax.experimental.pallas import tpu as pltpu
from jax.sharding import Mesh, PartitionSpec as P

K = 29
SPAN = 8
STEPS = (-2, -1, 1, 2)
BLOCKS_AT = (0, 7, 13, 19, 24, 29)
F32 = jnp.float32
BF16 = jnp.bfloat16
ALL = ("z", "x", "core")


def params(mib):
    return pltpu.CompilerParams(vmem_limit_bytes=mib * 1024 * 1024)


def dot(a, b):
    return jnp.dot(a, b, preferred_element_type=F32)


def iota(shape, dim):
    return lax.broadcasted_iota(jnp.int32, shape, dim)


def hot(cond):
    return jnp.where(cond, 1.0, 0.0).astype(BF16)


def column(row):
    n = row.shape[1]
    eye = iota((n, n), 0) == iota((n, n), 1)
    return jnp.sum(jnp.where(eye, row.astype(F32), 0.0), axis=1, keepdims=True)


def dp_index(n_x):
    return (lax.axis_index("z") * n_x + lax.axis_index("x")) * 2 + lax.axis_index("core")


def prep_kernel(me_ref, owner_ref, dst_ref, *outs):
    req_refs, take_ref, put_ref = outs[:4], outs[4], outs[5]
    n = owner_ref.shape[0]
    cap = n // 4
    off = (owner_ref[...] - me_ref[0]).astype(F32)
    eye = iota((n, n), 0) == iota((n, n), 1)
    off_row = jnp.sum(jnp.where(eye, off, 0.0), axis=0, keepdims=True)
    dst_row = dst_ref[...].astype(F32)
    dst = column(dst_ref[...])
    same = off == off_row
    earlier = same & (iota((n, n), 1) < iota((n, n), 0))
    pos = jnp.sum(jnp.where(earlier, 1.0, 0.0), axis=1, keepdims=True)
    before = same & (iota((n, n), 0) < iota((n, n), 1))
    pos_row = jnp.sum(jnp.where(before, 1.0, 0.0), axis=0, keepdims=True)
    base, base_row = jnp.full_like(off, -1000.0), jnp.full_like(off_row, -1000.0)
    for q, step in enumerate(STEPS):
        base = jnp.where(off == step, float(q * cap), base)
        base_row = jnp.where(off_row == step, float(q * cap), base_row)
        mine = (off == step) & (pos == iota((n, cap), 1).astype(F32))
        ids = jnp.sum(jnp.where(mine, dst + 1.0, 0.0), axis=0, keepdims=True)
        req_refs[q][...] = ids.astype(jnp.int32)
    slot, slot_row = base + pos, base_row + pos_row
    lanes = iota((n, n), 1).astype(F32)
    rows = iota((n, n), 0).astype(F32)
    take_ref[:, :n] = hot((off == 0.0) & (dst == lanes))
    take_ref[:, n:] = hot(slot == lanes)
    put_ref[:n, :] = hot((off_row == 0.0) & (dst_row == rows))
    put_ref[n:, :] = hot(slot_row == rows)


def serve_kernel(r0, r1, r2, r3, grad_ref, o0, o1, o2, o3):
    n = grad_ref.shape[0]
    cap = r0.shape[1]
    for r, o in ((r0, o0), (r1, o1), (r2, o2), (r3, o3)):
        pick = hot(iota((n, cap), 0) + 1 == r[...])
        o[...] = lax.dot_general(
            pick, grad_ref[...], (((0,), (0,)), ((), ())), preferred_element_type=F32
        ).astype(BF16)


def turn(mats_ref, src_ref, res_ref):
    n = src_ref.shape[1]
    for g in range(n // 8):
        rhs = src_ref[:, 8 * g : 8 * g + 8, :].reshape(256, 128).astype(BF16)
        res = dot(mats_ref[g], rhs)
        res_ref[:, 8 * g : 8 * g + 8, :] = res.reshape(30, 8, 128)


def build(table_ref, rot_hot, mats_ref, tmp_ref):
    n = rot_hot.shape[0]
    n_rot = rot_hot.shape[1]
    spread = hot(iota((K, 256), 1) // 8 == iota((K, 256), 0))
    wide = dot(table_ref[...], spread).astype(BF16)
    own = (iota((n, 256), 1) % 8) == (iota((n, 256), 0) % 8)
    for k in range(K):
        tmp_ref[k] = jnp.where(own, dot(rot_hot, wide[k * n_rot : (k + 1) * n_rot]), 0.0)
    tmp_ref[K] = jnp.zeros((n, 256), F32)
    for g in range(n // 8):
        mats_ref[g] = tmp_ref[:, 8 * g : 8 * g + 8, :].reshape(240, 256).astype(BF16)


def fill(dst_ref, j, wide):
    for i in range(wide.shape[1] // 128):
        dst_ref[j + i] = wide[:, 128 * i : 128 * i + 128]


def chunks():
    j = 0
    while j < K:
        w = min(4, K - j)
        yield j, w
        j += w


def source_kernel(
    src_ref, rot_ref, tab_ref, tabt_ref, feats_ref, mats_ref, matst_ref, h_ref, ht_ref,
    tmp_ref, in_ref, res_ref,
):
    n = feats_ref.shape[0]
    n_rot = tab_ref.shape[0] // K
    rot_hot = hot(column(rot_ref[...]) == iota((n, n_rot), 1).astype(F32))
    src_hot = hot(column(src_ref[...]) == iota((n, n), 1).astype(F32))
    for j, w in chunks():
        fill(in_ref, j, dot(src_hot, feats_ref[:, j * 128 : (j + w) * 128]))
    for j in range(K, 32):
        in_ref[j] = jnp.zeros((n, 128), F32)
    build(tab_ref, rot_hot, mats_ref, tmp_ref)
    turn(mats_ref, in_ref, res_ref)
    for k in range(K):
        h_ref[:, k * 128 : (k + 1) * 128] = res_ref[k].astype(BF16)
        ht_ref[k * 128 : (k + 1) * 128, :] = res_ref[k].T.astype(BF16)
    build(tabt_ref, rot_hot, matst_ref, tmp_ref)


def upstream_kernel(take_ref, mats_ref, grad_ref, r0, r1, r2, r3, u_ref, in_ref, res_ref):
    n = grad_ref.shape[0]
    for j, w in chunks():
        cols = slice(j * 128, (j + w) * 128)
        rows = jnp.concatenate([grad_ref[:, cols]] + [r[:, cols] for r in (r0, r1, r2, r3)], axis=0)
        fill(in_ref, j, dot(take_ref[...], rows))
    for j in range(K, 32):
        in_ref[j] = jnp.zeros((n, 128), F32)
    turn(mats_ref, in_ref, res_ref)
    for k in range(K):
        u_ref[:, k * 128 : (k + 1) * 128] = res_ref[k].astype(BF16)


def rank(n_z, z, target):
    order = sorted(range(n_z), key=lambda t: (-abs(t - z), -t))
    return order.index(target)


def by_rank(n_z, i):
    return [next(t for t in range(n_z) if rank(n_z, z, t) == i) for z in range(n_z)]


def choose(z, values):
    out = jnp.int32(values[0])
    for at in range(1, len(values)):
        out = jnp.where(z == at, jnp.int32(values[at]), out)
    return out


def grad_kernel(n_z, n_x, pos_ref, hta, htb, ua, ub, *outs_and_scratch):
    outs, flat = outs_and_scratch[:-1], outs_and_scratch[-1]
    z, x, core = pos_ref[0], pos_ref[1], pos_ref[2]

    def left(first, start, size):
        at = slice(first * 128 + start, first * 128 + start + size)
        return [hta[at, :], htb[at, :]]

    def right(first, width):
        at = slice(first * 128, (first + width) * 128)
        return [ua[:, at], ub[:, at]]

    def emit(base, width, start, res):
        for b in range(width):
            flat[pl.ds(base + start * width + b, res.shape[0], stride=width), :] = res[
                :, b * 128 : (b + 1) * 128
            ]

    base = 0
    rows0 = jnp.concatenate(right(0, 7), axis=0)
    for i in range(7):
        emit(base, 7, 128 * i, dot(jnp.concatenate(left(0, 128 * i, 128), axis=1), rows0))
    base += 49 * 128
    for first, width in ((7, 6), (19, 5)):
        real, imag = right(first, width), right(first + width, width)
        same = jnp.concatenate(real + imag, axis=0)
        cross = jnp.concatenate(imag + [-v for v in real], axis=0)
        for i in range(width):
            lhs = jnp.concatenate(
                left(first, 128 * i, 128) + left(first + width, 128 * i, 128), axis=1
            )
            emit(base, width, 128 * i, dot(lhs, same))
            emit(base + width * width * 128, width, 128 * i, dot(lhs, cross))
        base += 2 * width * width * 128

    rows = outs[0].shape[0]
    at_out = 0
    for o in list(range(1, n_x)) + [0]:
        for i in range(n_z):
            target = choose(z, by_rank(n_z, i))
            start = ((target * n_x + (x + o) % n_x) * 2 + core) * rows
            if rows % 8 == 0:
                start = pl.multiple_of(start, 8)
            ref = outs[at_out]
            ref[...] = flat[pl.ds(start, rows), :].astype(ref.dtype)
            at_out += 1


def message_kernel(n_half, rows, core_ref, wa, wb, h_ref, matst_ref, put_ref, *rest):
    local_ref, outs = rest[0], rest[1:5]
    flat, in_ref, res_ref, wide_ref = rest[5:]
    n = h_ref.shape[0]
    cap = n // 4
    piece = wa.shape[1]
    core = core_ref[0]
    for ref, who in ((wa, core), (wb, 1 - core)):
        for p in range(wa.shape[0]):
            half, chip = divmod(p, wa.shape[0] // n_half)
            start = (chip * 2 + who) * rows + half * (rows - piece)
            if rows % 8 == 0:
                start = pl.multiple_of(start, 8)
            flat[pl.ds(start, piece), :] = ref[p].astype(F32)

    def weight(base, width, b, many):
        parts = [
            flat[pl.ds(base + b + t, width * 128, stride=width), :].astype(BF16)
            for t in range(many)
        ]
        return parts[0] if many == 1 else jnp.concatenate(parts, axis=1)

    def rounded(v):
        return v.astype(BF16).astype(F32)

    def pairs(width):
        return [(b, min(2, width - b)) for b in range(0, width, 2)]

    for b, many in pairs(7):
        fill(in_ref, b, rounded(dot(h_ref[:, : 7 * 128], weight(0, 7, b, many))))
    base = 49 * 128
    for first, width in ((7, 6), (19, 5)):
        mid, end = (first + width) * 128, (first + 2 * width) * 128
        both = jnp.concatenate([h_ref[:, first * 128 : mid], h_ref[:, mid:end]], axis=0)
        for b, many in pairs(width):
            real = dot(both, weight(base, width, b, many))
            imag = dot(both, weight(base + width * width * 128, width, b, many))
            fill(in_ref, first + b, rounded(real[:n] - imag[n:]))
            fill(in_ref, first + width + b, rounded(imag[:n] + real[n:]))
        base += 2 * width * width * 128
    for j in range(K, 32):
        in_ref[j] = jnp.zeros((n, 128), F32)
    turn(matst_ref, in_ref, res_ref)
    for k in range(K):
        wide_ref[:, k * 128 : (k + 1) * 128] = res_ref[k].astype(BF16)
    for j, w in chunks():
        cols = slice(j * 128, (j + w) * 128)
        res = dot(put_ref[...], wide_ref[:, cols])
        local_ref[:, cols] = res[:n]
        for q in range(4):
            outs[q][:, cols] = res[n + q * cap : n + (q + 1) * cap].astype(BF16)


def collect_kernel(local_ref, r0, r1, r2, r3, m0, m1, m2, m3, out_ref):
    n = local_ref.shape[0]
    cap = r0.shape[1]
    hots = [hot(iota((n, cap), 0) + 1 == r[...]) for r in (r0, r1, r2, r3)]
    for j, w in chunks():
        cols = slice(j * 128, (j + w) * 128)
        total = local_ref[:, cols]
        for pick, m in zip(hots, (m0, m1, m2, m3)):
            total = total + dot(pick, m[:, cols])
        out_ref[:, cols] = total.astype(BF16)


def shape(dims, kind):
    return jax.ShapeDtypeStruct(dims, kind)


def on_device(
    n_z, n_x, node_feats, node_grad, flat_params, rot_table, edge_src, edge_dst, edge_rot,
    edge_owner,
):
    n = edge_src.shape[0]
    cap = n // 4
    width = node_feats.shape[1]
    rows = flat_params.shape[0]
    n_dp = n_z * n_x * 2
    n_rot = rot_table.shape[0]
    groups = lax.axis_size("groups")
    group, z, x, core = (lax.axis_index(a) for a in ("groups", "z", "x", "core"))
    me = dp_index(n_x)
    vmem = pl.BlockSpec(memory_space=pltpu.VMEM)
    smem = pl.BlockSpec(memory_space=pltpu.SMEM)

    def shift(block, step):
        route = [
            (i, i + step) for i in range(n_dp)
            if 0 <= i + step and i // SPAN == (i + step) // SPAN
        ]
        return lax.ppermute(block, ALL, route)

    def swap(block):
        return lax.ppermute(block, "core", [(0, 1), (1, 0)])

    piece = -(-rows // (16 * groups)) * 16
    part = lax.dynamic_slice_in_dim(flat_params, group * (rows - piece), piece, 0)
    w_own = lax.all_gather(part, ("groups", "z", "x"), axis=0)
    w_other = swap(w_own)

    row = lambda v: v.reshape(1, n)
    *req, take, put = pl.pallas_call(
        prep_kernel,
        out_shape=[shape((1, cap), jnp.int32)] * 4 + [shape((n, 2 * n), BF16), shape((2 * n, n), BF16)],
        in_specs=[smem, vmem, vmem],
        out_specs=[vmem] * 6,
        name="slots",
    )(me.reshape(1), edge_owner, row(edge_dst))
    got = [shift(r, s) for r, s in zip(req, STEPS)]
    served = pl.pallas_call(
        serve_kernel,
        out_shape=[shape((cap, width), BF16)] * 4,
        in_specs=[vmem] * 5,
        out_specs=[vmem] * 4,
        compiler_params=params(32),
        name="serve",
    )(*got, node_grad)
    back = [shift(r, -s) for r, s in zip(served, STEPS)]

    tab = rot_table.transpose(1, 0, 2).reshape(K * n_rot, K)
    tabt = rot_table.transpose(2, 0, 1).reshape(K * n_rot, K)
    mats, matst, h, ht = pl.pallas_call(
        source_kernel,
        out_shape=[
            shape((n // 8, 240, 256), BF16), shape((n // 8, 240, 256), BF16),
            shape((n, width), BF16), shape((width, n), BF16),
        ],
        in_specs=[vmem] * 5,
        out_specs=[vmem] * 4,
        scratch_shapes=[
            pltpu.VMEM((30, n, 256), F32), pltpu.VMEM((32, n, 128), F32),
            pltpu.VMEM((30, n, 128), F32),
        ],
        compiler_params=params(40),
        name="source",
    )(row(edge_src), row(edge_rot), tab, tabt, node_feats)
    ht_other = swap(ht)
    u = pl.pallas_call(
        upstream_kernel,
        out_shape=shape((n, width), BF16),
        in_specs=[vmem] * 7,
        out_specs=vmem,
        scratch_shapes=[pltpu.VMEM((32, n, 128), F32), pltpu.VMEM((30, n, 128), F32)],
        compiler_params=params(32),
        name="upstream",
    )(take, mats, node_grad, *back)
    u_other = swap(u)

    n_send = n_z * (n_x - 1)
    blocks = pl.pallas_call(
        lambda *refs: grad_kernel(n_z, n_x, *refs),
        out_shape=[shape((rows, 128), BF16)] * n_send + [shape((rows, 128), F32)] * n_z,
        in_specs=[smem] + [vmem] * 4,
        out_specs=[vmem] * (n_send + n_z),
        scratch_shapes=[pltpu.VMEM((rows * n_dp, 128), F32)],
        compiler_params=params(48),
        name="weight_terms",
    )(jnp.stack([z, x, core]), ht, ht_other, u, u_other)
    sums = []
    for i in range(n_z):
        total = blocks[n_send + i]
        for o in range(1, n_x):
            got_part = lax.ppermute(
                blocks[(o - 1) * n_z + i], "x", [(s, (s + o) % n_x) for s in range(n_x)]
            )
            total = total + got_part.astype(F32)
        sums.append(total)
    result = sums[n_z - 1]
    for way in (1, -1):
        arrived = None
        for k in range(n_z - 1, 0, -1):
            senders = [s for s in range(n_z) if 0 <= s + way * k < n_z]
            term = sums[rank(n_z, senders[0], senders[0] + way * k)]
            for s in senders[1:]:
                term = jnp.where(z == s, sums[rank(n_z, s, s + way * k)], term)
            if arrived is not None:
                term = term + arrived.astype(F32)
            arrived = lax.ppermute(term.astype(BF16), "z", [(s, s + way) for s in senders])
        if arrived is not None:
            result = result + arrived.astype(F32)
    weight_grad = result * (1.0 / math.sqrt(n * n_dp))

    local, *outbound = pl.pallas_call(
        lambda *refs: message_kernel(groups, rows, *refs),
        out_shape=[shape((n, width), F32)] + [shape((cap, width), BF16)] * 4,
        in_specs=[smem] + [vmem] * 5,
        out_specs=[vmem] * 5,
        scratch_shapes=[
            pltpu.VMEM((rows * n_dp, 128), F32), pltpu.VMEM((32, n, 128), F32),
            pltpu.VMEM((30, n, 128), F32), pltpu.VMEM((n, width), BF16),
        ],
        compiler_params=params(48),
        name="messages",
    )(core.reshape(1), w_own, w_other, h, matst, put)
    arrived = [shift(m, s) for m, s in zip(outbound, STEPS)]
    node_out = pl.pallas_call(
        collect_kernel,
        out_shape=shape((n, width), BF16),
        in_specs=[vmem] * 9,
        out_specs=vmem,
        compiler_params=params(32),
        name="collect",
    )(local, *got, *arrived)
    return (node_out, weight_grad)


def chips(mesh):
    n_dp = mesh.shape["dp"]
    line = list(mesh.devices.reshape(-1, n_dp)[0])
    coords = [getattr(d, "coords", None) for d in line]
    n_x = 2 if coords[0] is None else len({c[0] for c in coords})
    return n_dp // (2 * n_x), n_x


def solution(mesh):
    n_z, n_x = chips(mesh)
    fine = Mesh(
        np.asarray(mesh.devices).reshape(mesh.shape["groups"], n_z, n_x, 2),
        ("groups", "z", "x", "core"),
    )
    every = ("groups",) + ALL
    placed = (
        P(every, None),
        P(every, None),
        P(ALL, None),
        P(),
        P(every),
        P(every),
        P(every),
        P(every, None),
    )
    return jax.shard_map(
        lambda *args: on_device(n_z, n_x, *args),
        mesh=fine,
        in_specs=placed,
        out_specs=(P(every, None), P(every, None)),
        check_vma=False,
    )
```

```python
import math

import jax
import jax.numpy as jnp
import numpy as np
from jax import lax
from jax.experimental import pallas as pl
from jax.experimental.pallas import tpu as pltpu
from jax.sharding import Mesh, PartitionSpec as P

K = 29
SPAN = 8
STEPS = (-2, -1, 1, 2)
F32 = jnp.float32
BF16 = jnp.bfloat16
ALL = ("z", "x", "core")


def params(mib):
    return pltpu.CompilerParams(vmem_limit_bytes=mib * 1024 * 1024)


def dot(a, b):
    return jnp.dot(a, b, preferred_element_type=F32)


def iota(shape, dim):
    return lax.broadcasted_iota(jnp.int32, shape, dim)


def hot(cond):
    return jnp.where(cond, 1.0, 0.0).astype(BF16)


def column(row):
    n = row.shape[1]
    eye = iota((n, n), 0) == iota((n, n), 1)
    return jnp.sum(jnp.where(eye, row.astype(F32), 0.0), axis=1, keepdims=True)


def dp_index(n_x):
    return (lax.axis_index("z") * n_x + lax.axis_index("x")) * 2 + lax.axis_index("core")


def send_kernel(me_ref, owner_ref, src_ref, dst_ref, rot_ref, feats_ref, *outs):
    n = feats_ref.shape[0]
    width = feats_ref.shape[1]
    half, cap = n // 2, n // 4
    off_row = (owner_ref[...] - me_ref[0]).astype(F32)
    off = column(off_row)
    before = (off == off_row) & (iota((n, n), 0) < iota((n, n), 1))
    slot = jnp.sum(jnp.where(before, 1.0, 0.0), axis=0, keepdims=True)
    for q, step in enumerate(STEPS):
        slot = jnp.where(off_row == step, slot + float(half + q * cap), slot)
    slots = half + 4 * cap
    here = slot == iota((slots, n), 0).astype(F32)

    def pick(row):
        return jnp.sum(jnp.where(here, row, 0.0), axis=1, keepdims=True)

    source = pick(src_ref[...].astype(F32) + 1.0) - 1.0
    target = pick(dst_ref[...].astype(F32) + 1.0)
    turns = pick(rot_ref[...].astype(F32))
    source_hot = hot(source == iota((slots, n), 1).astype(F32))
    lane = iota((slots, 128), 1)
    ids = jnp.where(lane == 0, target, jnp.where(lane == 1, turns, 0.0)).astype(BF16)
    spans = [(0, half)] + [(half + q * cap, cap) for q in range(4)]
    for o, (at, size) in zip(outs, spans):
        o[:, width:] = ids[at : at + size]
    for j, w in chunks():
        cols = slice(j * 128, (j + w) * 128)
        rows = dot(source_hot, feats_ref[:, cols]).astype(BF16)
        for o, (at, size) in zip(outs, spans):
            o[:, cols] = rows[at : at + size]


def turn(mats_ref, src_ref, res_ref):
    lanes = src_ref.shape[2]
    for g in range(src_ref.shape[1] // 8):
        rhs = src_ref[:, 8 * g : 8 * g + 8, :].reshape(256, lanes).astype(BF16)
        res = dot(mats_ref[g], rhs)
        res_ref[:, 8 * g : 8 * g + 8, :] = res.reshape(30, 8, lanes)


def build(table_ref, rot_hot, mats_ref, tmp_ref):
    n = rot_hot.shape[0]
    n_rot = rot_hot.shape[1]
    spread = hot(iota((K, 256), 1) // 8 == iota((K, 256), 0))
    wide = dot(table_ref[...], spread).astype(BF16)
    own = (iota((n, 256), 1) % 8) == (iota((n, 256), 0) % 8)
    for k in range(K):
        tmp_ref[k] = jnp.where(own, dot(rot_hot, wide[k * n_rot : (k + 1) * n_rot]), 0.0)
    tmp_ref[K] = jnp.zeros((n, 256), F32)
    for g in range(n // 8):
        mats_ref[g] = tmp_ref[:, 8 * g : 8 * g + 8, :].reshape(240, 256).astype(BF16)


def chunks():
    j = 0
    while j < K:
        w = min(4, K - j)
        yield j, w
        j += w


def joined(refs, cols):
    return jnp.concatenate([r[:, cols] for r in refs], axis=0)


def number(ids, lane):
    at = iota(ids.shape, 1) == lane
    return jnp.sum(jnp.where(at, ids.astype(F32), 0.0), axis=1, keepdims=True)


def rotate_kernel(count, *refs):
    raw, (tab_ref, tabt_ref, grad_ref) = refs[:count], refs[count : count + 3]
    both_ref, matst_ref, hot_ref, mats_ref, tmp_ref, in_ref, res_ref = refs[count + 3 :]
    n = grad_ref.shape[0]
    n_rot = tab_ref.shape[0] // K
    width = grad_ref.shape[1]
    ids = joined(raw, slice(width, width + 128))
    slots = ids.shape[0]
    target_hot = hot(number(ids, 0) - 1.0 == iota((slots, n), 1).astype(F32))
    rot_hot = hot(number(ids, 1) == iota((slots, n_rot), 1).astype(F32))
    hot_ref[...] = target_hot
    for j, w in chunks():
        cols = slice(j * 128, (j + w) * 128)
        rows = joined(raw, cols).astype(F32)
        back = dot(target_hot, grad_ref[:, cols])
        for i in range(w):
            in_ref[j + i, :, :128] = rows[:, 128 * i : 128 * i + 128]
            in_ref[j + i, :, 128:] = back[:, 128 * i : 128 * i + 128]
    for j in range(K, 32):
        in_ref[j] = jnp.zeros((slots, 256), F32)
    build(tab_ref, rot_hot, mats_ref, tmp_ref)
    turn(mats_ref, in_ref, res_ref)
    for k in range(K):
        cols = slice(k * 128, (k + 1) * 128)
        both_ref[:slots, cols] = res_ref[k, :, :128].astype(BF16)
        both_ref[slots:, cols] = res_ref[k, :, 128:].astype(BF16)
    build(tabt_ref, rot_hot, matst_ref, tmp_ref)


def rank(n_z, z, target):
    order = sorted(range(n_z), key=lambda t: (-abs(t - z), -t))
    return order.index(target)


def by_rank(n_z, i):
    return [next(t for t in range(n_z) if rank(n_z, z, t) == i) for z in range(n_z)]


def choose(z, values):
    out = jnp.int32(values[0])
    for at in range(1, len(values)):
        out = jnp.where(z == at, jnp.int32(values[at]), out)
    return out


def grad_kernel(n_z, n_x, pos_ref, *refs):
    parts, outs, flat = refs[:4], refs[4:-1], refs[-1]
    z, x, core = pos_ref[0], pos_ref[1], pos_ref[2]

    def left(first):
        at = slice(first * 128, (first + 1) * 128)
        return [p[: p.shape[0] // 2, at] for p in parts]

    def right(first, width):
        at = slice(first * 128, (first + width) * 128)
        return [p[p.shape[0] // 2 :, at] for p in parts]

    def outer(lhs, rhs):
        return lax.dot_general(lhs, rhs, (((0,), (0,)), ((), ())), preferred_element_type=F32)

    def emit(base, width, start, res):
        for b in range(width):
            flat[pl.ds(base + start * width + b, res.shape[0], stride=width), :] = res[
                :, b * 128 : (b + 1) * 128
            ]

    rows0 = jnp.concatenate(right(0, 7), axis=0)
    for i in range(7):
        emit(0, 7, 128 * i, outer(jnp.concatenate(left(i), axis=0), rows0))
    base = 49 * 128
    for first, width in ((7, 6), (19, 5)):
        real, imag = right(first, width), right(first + width, width)
        same = jnp.concatenate(real + imag, axis=0)
        cross = jnp.concatenate(imag + [-v for v in real], axis=0)
        for i in range(width):
            lhs = jnp.concatenate(left(first + i) + left(first + width + i), axis=0)
            emit(base, width, 128 * i, outer(lhs, same))
            emit(base + width * width * 128, width, 128 * i, outer(lhs, cross))
        base += 2 * width * width * 128

    rows = outs[0].shape[0]
    at_out = 0
    for o in list(range(1, n_x)) + [0]:
        for i in range(n_z):
            target = choose(z, by_rank(n_z, i))
            start = ((target * n_x + (x + o) % n_x) * 2 + core) * rows
            if rows % 8 == 0:
                start = pl.multiple_of(start, 8)
            ref = outs[at_out]
            ref[...] = flat[pl.ds(start, rows), :].astype(ref.dtype)
            at_out += 1


def message_kernel(w_ref, *refs):
    both, mats, hots = refs[0:2], refs[2:4], refs[4:6]
    out_ref, flat, in_ref, res_ref, wide_ref = refs[6:]
    n = out_ref.shape[0]
    slots = in_ref.shape[1]
    part = w_ref.shape[0] // 16
    for p in range(16):
        flat[p * part : (p + 1) * part, :] = w_ref[p * part : (p + 1) * part, :].astype(F32)

    def h(first, end):
        return jnp.concatenate(
            [r[: r.shape[0] // 2, first * 128 : end * 128] for r in both], axis=0
        )

    def fill(j, wide):
        for i in range(wide.shape[1] // 128):
            in_ref[j + i] = wide[:, 128 * i : 128 * i + 128]

    def weight(base, width, b, many):
        parts = [
            flat[pl.ds(base + b + t, width * 128, stride=width), :].astype(BF16)
            for t in range(many)
        ]
        return parts[0] if many == 1 else jnp.concatenate(parts, axis=1)

    def rounded(v):
        return v.astype(BF16).astype(F32)

    def pairs(width):
        return [(b, min(2, width - b)) for b in range(0, width, 2)]

    h0 = h(0, 7)
    for b, many in pairs(7):
        fill(b, rounded(dot(h0, weight(0, 7, b, many))))
    base = 49 * 128
    for first, width in ((7, 6), (19, 5)):
        mid, end = first + width, first + 2 * width
        pair = jnp.concatenate([h(first, mid), h(mid, end)], axis=0)
        for b, many in pairs(width):
            real = dot(pair, weight(base, width, b, many))
            imag = dot(pair, weight(base + width * width * 128, width, b, many))
            fill(first + b, rounded(real[:slots] - imag[slots:]))
            fill(mid + b, rounded(imag[:slots] + real[slots:]))
        base += 2 * width * width * 128
    for j in range(K, 32):
        in_ref[j] = jnp.zeros((slots, 128), F32)
    at = 0
    for m in mats:
        size = m.shape[0] * 8
        turn(m, in_ref.at[:, at : at + size, :], res_ref.at[:, at : at + size, :])
        at += size
    for k in range(K):
        wide_ref[:, k * 128 : (k + 1) * 128] = res_ref[k].astype(BF16)
    target = jnp.concatenate([r[...] for r in hots], axis=0).astype(F32).T.astype(BF16)
    for j, w in chunks():
        cols = slice(j * 128, (j + w) * 128)
        out_ref[:, cols] = dot(target, wide_ref[:, cols]).astype(BF16)


def shape(dims, kind):
    return jax.ShapeDtypeStruct(dims, kind)


def on_device(
    n_z, n_x, node_feats, node_grad, flat_params, rot_table, edge_src, edge_dst, edge_rot,
    edge_owner,
):
    n = edge_src.shape[0]
    cap = n // 4
    width = node_feats.shape[1]
    rows = flat_params.shape[0]
    n_dp = n_z * n_x * 2
    n_rot = rot_table.shape[0]
    z, x, core = (lax.axis_index(a) for a in ALL)
    me = dp_index(n_x)
    vmem = pl.BlockSpec(memory_space=pltpu.VMEM)
    smem = pl.BlockSpec(memory_space=pltpu.SMEM)

    def shift(block, step):
        route = [
            (i, i + step) for i in range(n_dp)
            if 0 <= i + step and i // SPAN == (i + step) // SPAN
        ]
        return lax.ppermute(block, ALL, route)

    def swap(block):
        return lax.ppermute(block, "core", [(0, 1), (1, 0)])

    weights = lax.all_gather(flat_params, ALL, axis=0, tiled=True)

    row = lambda v: v.reshape(1, n)
    here, *outbound = pl.pallas_call(
        send_kernel,
        out_shape=[shape((n // 2, width + 128), BF16)] + [shape((cap, width + 128), BF16)] * 4,
        in_specs=[smem] + [vmem] * 5,
        out_specs=[vmem] * 5,
        compiler_params=params(32),
        name="send",
    )(me.reshape(1), row(edge_owner), row(edge_src), row(edge_dst), row(edge_rot), node_feats)
    arrived = [shift(r, s) for r, s in zip(outbound, STEPS)]

    tab = rot_table.transpose(1, 0, 2).reshape(K * n_rot, K)
    tabt = rot_table.transpose(2, 0, 1).reshape(K * n_rot, K)

    def rotate(rows_in, name):
        slots = sum(r.shape[0] for r in rows_in)
        return pl.pallas_call(
            lambda *refs: rotate_kernel(len(rows_in), *refs),
            out_shape=[
                shape((2 * slots, width), BF16), shape((slots // 8, 240, 256), BF16),
                shape((slots, n), BF16),
            ],
            in_specs=[vmem] * (len(rows_in) + 3),
            out_specs=[vmem] * 3,
            scratch_shapes=[
                pltpu.VMEM((slots // 8, 240, 256), BF16), pltpu.VMEM((30, slots, 256), F32),
                pltpu.VMEM((32, slots, 256), F32), pltpu.VMEM((30, slots, 256), F32),
            ],
            compiler_params=params(40),
            name=name,
        )(*rows_in, tab, tabt, node_grad)

    both_near, matst_near, hot_near = rotate([here], "rotate_near")
    both_near_other = swap(both_near)
    both_far, matst_far, hot_far = rotate(arrived, "rotate_far")
    both_far_other = swap(both_far)

    n_send = n_z * (n_x - 1)
    blocks = pl.pallas_call(
        lambda *refs: grad_kernel(n_z, n_x, *refs),
        out_shape=[shape((rows, 128), BF16)] * n_send + [shape((rows, 128), F32)] * n_z,
        in_specs=[smem] + [vmem] * 4,
        out_specs=[vmem] * (n_send + n_z),
        scratch_shapes=[pltpu.VMEM((rows * n_dp, 128), F32)],
        compiler_params=params(48),
        name="weight_terms",
    )(jnp.stack([z, x, core]), both_near, both_near_other, both_far, both_far_other)
    sums = []
    for i in range(n_z):
        total = blocks[n_send + i]
        for o in range(1, n_x):
            got_part = lax.ppermute(
                blocks[(o - 1) * n_z + i], "x", [(s, (s + o) % n_x) for s in range(n_x)]
            )
            total = total + got_part.astype(F32)
        sums.append(total)
    result = sums[n_z - 1]
    for way in (1, -1):
        arrived = None
        for k in range(n_z - 1, 0, -1):
            senders = [s for s in range(n_z) if 0 <= s + way * k < n_z]
            term = sums[rank(n_z, senders[0], senders[0] + way * k)]
            for s in senders[1:]:
                term = jnp.where(z == s, sums[rank(n_z, s, s + way * k)], term)
            if arrived is not None:
                term = term + arrived.astype(F32)
            term = term.astype(BF16)
            arrived = lax.ppermute(term, "z", [(s, s + way) for s in senders])
        if arrived is not None:
            result = result + arrived.astype(F32)
    weight_grad = result * (1.0 / math.sqrt(n * n_dp))

    weights, _ = lax.optimization_barrier((weights, term))
    slots = n // 2 + 4 * cap
    node_out = pl.pallas_call(
        message_kernel,
        out_shape=shape((n, width), BF16),
        in_specs=[vmem] * 7,
        out_specs=vmem,
        scratch_shapes=[
            pltpu.VMEM((rows * n_dp, 128), F32), pltpu.VMEM((32, slots, 128), F32),
            pltpu.VMEM((30, slots, 128), F32), pltpu.VMEM((slots, width), BF16),
        ],
        compiler_params=params(48),
        name="messages",
    )(weights, both_near, both_far, matst_near, matst_far, hot_near, hot_far)
    return (node_out, weight_grad)


def chips(mesh):
    n_dp = mesh.shape["dp"]
    line = list(mesh.devices.reshape(-1, n_dp)[0])
    coords = [getattr(d, "coords", None) for d in line]
    n_x = 2 if coords[0] is None else len({c[0] for c in coords})
    return n_dp // (2 * n_x), n_x


def solution(mesh):
    n_z, n_x = chips(mesh)
    fine = Mesh(
        np.asarray(mesh.devices).reshape(mesh.shape["groups"], n_z, n_x, 2),
        ("groups", "z", "x", "core"),
    )
    every = ("groups",) + ALL
    placed = (
        P(every, None),
        P(every, None),
        P(ALL, None),
        P(),
        P(every),
        P(every),
        P(every),
        P(every, None),
    )
    return jax.shard_map(
        lambda *args: on_device(n_z, n_x, *args),
        mesh=fine,
        in_specs=placed,
        out_specs=(P(every, None), P(every, None)),
        check_vma=False,
    )
```

```python
import math

import jax
import jax.numpy as jnp
import numpy as np
from jax import lax
from jax.experimental import pallas as pl
from jax.experimental.pallas import tpu as pltpu
from jax.sharding import Mesh, PartitionSpec as P

K = 29
SPAN = 8
STEPS = (-2, -1, 1, 2)
F32 = jnp.float32
BF16 = jnp.bfloat16
ALL = ("z", "x", "core")


def dot(a, b):
    return jnp.dot(a, b, preferred_element_type=F32)


def iota(shape, dim):
    return lax.broadcasted_iota(jnp.int32, shape, dim)


def hot(cond):
    return jnp.where(cond, 1.0, 0.0).astype(BF16)


def column(row):
    n = row.shape[1]
    eye = iota((n, n), 0) == iota((n, n), 1)
    return jnp.sum(jnp.where(eye, row.astype(F32), 0.0), axis=1, keepdims=True)


def dp_index(n_x):
    return (lax.axis_index("z") * n_x + lax.axis_index("x")) * 2 + lax.axis_index("core")


def send_kernel(me_ref, owner_ref, src_ref, dst_ref, rot_ref, feats_ref, *outs):
    n = feats_ref.shape[0]
    width = feats_ref.shape[1]
    half, cap = n // 2, n // 4
    off_row = (owner_ref[...] - me_ref[0]).astype(F32)
    off = column(off_row)
    before = (off == off_row) & (iota((n, n), 0) < iota((n, n), 1))
    slot = jnp.sum(jnp.where(before, 1.0, 0.0), axis=0, keepdims=True)
    for q, step in enumerate(STEPS):
        slot = jnp.where(off_row == step, slot + float(half + q * cap), slot)
    slots = half + 4 * cap
    here = slot == iota((slots, n), 0).astype(F32)

    def pick(row):
        return jnp.sum(jnp.where(here, row, 0.0), axis=1, keepdims=True)

    source = pick(src_ref[...].astype(F32) + 1.0) - 1.0
    target = pick(dst_ref[...].astype(F32) + 1.0)
    turns = pick(rot_ref[...].astype(F32))
    source_hot = hot(source == iota((slots, n), 1).astype(F32))
    lane = iota((slots, 128), 1)
    ids = jnp.where(lane == 0, target, jnp.where(lane == 1, turns, 0.0)).astype(BF16)
    spans = [(0, half)] + [(half + q * cap, cap) for q in range(4)]
    for o, (at, size) in zip(outs, spans):
        o[:, width:] = ids[at : at + size]
    for j, w in chunks():
        cols = slice(j * 128, (j + w) * 128)
        rows = dot(source_hot, feats_ref[:, cols]).astype(BF16)
        for o, (at, size) in zip(outs, spans):
            o[:, cols] = rows[at : at + size]


def turn(mats_ref, src_ref, res_ref):
    lanes = src_ref.shape[2]
    for g in range(src_ref.shape[1] // 8):
        rhs = src_ref[:, 8 * g : 8 * g + 8, :].reshape(256, lanes).astype(BF16)
        res = dot(mats_ref[g], rhs)
        res_ref[:, 8 * g : 8 * g + 8, :] = res.reshape(30, 8, lanes)


def build(table_ref, rot_hot, mats_ref, tmp_ref):
    n = rot_hot.shape[0]
    n_rot = rot_hot.shape[1]
    spread = hot(iota((K, 256), 1) // 8 == iota((K, 256), 0))
    wide = dot(table_ref[...], spread).astype(BF16)
    own = (iota((n, 256), 1) % 8) == (iota((n, 256), 0) % 8)
    for k in range(K):
        tmp_ref[k] = jnp.where(own, dot(rot_hot, wide[k * n_rot : (k + 1) * n_rot]), 0.0)
    tmp_ref[K] = jnp.zeros((n, 256), F32)
    for g in range(n // 8):
        mats_ref[g] = tmp_ref[:, 8 * g : 8 * g + 8, :].reshape(240, 256).astype(BF16)


def chunks():
    j = 0
    while j < K:
        w = min(4, K - j)
        yield j, w
        j += w


def joined(refs, cols):
    return jnp.concatenate([r[:, cols] for r in refs], axis=0)


def number(ids, lane):
    at = iota(ids.shape, 1) == lane
    return jnp.sum(jnp.where(at, ids.astype(F32), 0.0), axis=1, keepdims=True)


def rotate_kernel(count, *refs):
    raw, (tab_ref, tabt_ref, grad_ref) = refs[:count], refs[count : count + 3]
    both_ref, matst_ref, hot_ref, mats_ref, tmp_ref, in_ref, res_ref = refs[count + 3 :]
    n = grad_ref.shape[0]
    n_rot = tab_ref.shape[0] // K
    width = grad_ref.shape[1]
    ids = joined(raw, slice(width, width + 128))
    slots = ids.shape[0]
    target_hot = hot(number(ids, 0) - 1.0 == iota((slots, n), 1).astype(F32))
    rot_hot = hot(number(ids, 1) == iota((slots, n_rot), 1).astype(F32))
    hot_ref[...] = target_hot
    for j, w in chunks():
        cols = slice(j * 128, (j + w) * 128)
        rows = joined(raw, cols).astype(F32)
        back = dot(target_hot, grad_ref[:, cols])
        for i in range(w):
            in_ref[j + i, :, :128] = rows[:, 128 * i : 128 * i + 128]
            in_ref[j + i, :, 128:] = back[:, 128 * i : 128 * i + 128]
    for j in range(K, 32):
        in_ref[j] = jnp.zeros((slots, 256), F32)
    build(tab_ref, rot_hot, mats_ref, tmp_ref)
    turn(mats_ref, in_ref, res_ref)
    for k in range(K):
        cols = slice(k * 128, (k + 1) * 128)
        both_ref[:slots, cols] = res_ref[k, :, :128].astype(BF16)
        both_ref[slots:, cols] = res_ref[k, :, 128:].astype(BF16)
    build(tabt_ref, rot_hot, matst_ref, tmp_ref)


def shifts(n_z):
    return sorted(range(n_z), key=lambda i: (i == 0, abs(i - n_z // 2)))


def grad_kernel(n_z, n_x, pos_ref, *refs):
    parts, outs, flat = refs[:4], refs[4:-1], refs[-1]
    z, x, core = pos_ref[0], pos_ref[1], pos_ref[2]

    def left(first):
        at = slice(first * 128, (first + 1) * 128)
        return [p[: p.shape[0] // 2, at] for p in parts]

    def right(first, width):
        at = slice(first * 128, (first + width) * 128)
        return [p[p.shape[0] // 2 :, at] for p in parts]

    def outer(lhs, rhs):
        return lax.dot_general(lhs, rhs, (((0,), (0,)), ((), ())), preferred_element_type=F32)

    def emit(base, width, start, res):
        for b in range(width):
            flat[pl.ds(base + start * width + b, res.shape[0], stride=width), :] = res[
                :, b * 128 : (b + 1) * 128
            ]

    rows0 = jnp.concatenate(right(0, 7), axis=0)
    for i in range(7):
        emit(0, 7, 128 * i, outer(jnp.concatenate(left(i), axis=0), rows0))
    base = 49 * 128
    for first, width in ((7, 6), (19, 5)):
        real, imag = right(first, width), right(first + width, width)
        same = jnp.concatenate(real + imag, axis=0)
        cross = jnp.concatenate(imag + [-v for v in real], axis=0)
        for i in range(width):
            lhs = jnp.concatenate(left(first + i) + left(first + width + i), axis=0)
            emit(base, width, 128 * i, outer(lhs, same))
            emit(base + width * width * 128, width, 128 * i, outer(lhs, cross))
        base += 2 * width * width * 128

    rows = outs[0].shape[0]
    at_out = 0
    for o in list(range(1, n_x)) + [0]:
        for i in shifts(n_z):
            start = (((z + i) % n_z * n_x + (x + o) % n_x) * 2 + core) * rows
            if rows % 8 == 0:
                start = pl.multiple_of(start, 8)
            ref = outs[at_out]
            ref[...] = flat[pl.ds(start, rows), :].astype(ref.dtype)
            at_out += 1


def message_kernel(rows, pos_ref, *refs):
    pieces, both, mats, hots = refs[:4], refs[4:6], refs[6:8], refs[8:10]
    out_ref, flat, in_ref, res_ref, wide_ref = refs[10:]
    n = out_ref.shape[0]
    slots = in_ref.shape[1]
    group, core = pos_ref[0], pos_ref[1]
    for at, ref in enumerate(pieces):
        which = group if at < 2 else 1 - group
        who = core if at % 2 == 0 else 1 - core
        size = ref.shape[1]
        for chip in range(ref.shape[0]):
            start = (chip * 2 + who) * rows + which * (rows - size)
            if rows % 8 == 0:
                start = pl.multiple_of(start, 8)
            flat[pl.ds(start, size), :] = ref[chip].astype(F32)

    def h(first, end):
        return jnp.concatenate(
            [r[: r.shape[0] // 2, first * 128 : end * 128] for r in both], axis=0
        )

    def fill(j, wide):
        for i in range(wide.shape[1] // 128):
            in_ref[j + i] = wide[:, 128 * i : 128 * i + 128]

    def weight(base, width, b, many):
        parts = [
            flat[pl.ds(base + b + t, width * 128, stride=width), :].astype(BF16)
            for t in range(many)
        ]
        return parts[0] if many == 1 else jnp.concatenate(parts, axis=1)

    def rounded(v):
        return v.astype(BF16).astype(F32)

    def pairs(width):
        return [(b, min(2, width - b)) for b in range(0, width, 2)]

    h0 = h(0, 7)
    for b, many in pairs(7):
        fill(b, rounded(dot(h0, weight(0, 7, b, many))))
    base = 49 * 128
    for first, width in ((7, 6), (19, 5)):
        mid, end = first + width, first + 2 * width
        pair = jnp.concatenate([h(first, mid), h(mid, end)], axis=0)
        for b, many in pairs(width):
            real = dot(pair, weight(base, width, b, many))
            imag = dot(pair, weight(base + width * width * 128, width, b, many))
            fill(first + b, rounded(real[:slots] - imag[slots:]))
            fill(mid + b, rounded(imag[:slots] + real[slots:]))
        base += 2 * width * width * 128
    for j in range(K, 32):
        in_ref[j] = jnp.zeros((slots, 128), F32)
    at = 0
    for m in mats:
        size = m.shape[0] * 8
        turn(m, in_ref.at[:, at : at + size, :], res_ref.at[:, at : at + size, :])
        at += size
    for k in range(K):
        wide_ref[:, k * 128 : (k + 1) * 128] = res_ref[k].astype(BF16)
    target = jnp.concatenate([r[...] for r in hots], axis=0).astype(F32).T.astype(BF16)
    for j, w in chunks():
        cols = slice(j * 128, (j + w) * 128)
        out_ref[:, cols] = dot(target, wide_ref[:, cols]).astype(BF16)


def shape(dims, kind):
    return jax.ShapeDtypeStruct(dims, kind)


def whole(like):
    zeros = (0,) * len(like.shape)
    return pl.BlockSpec(like.shape, lambda i: zeros, pipeline_mode=pl.Buffered(1))


def call(kernel, name, mib, outs, operands, scratch=(), numbers=None):
    first = [] if numbers is None else [pl.BlockSpec(memory_space=pltpu.SMEM)]
    return pl.pallas_call(
        kernel,
        grid=(1,),
        out_shape=outs,
        in_specs=first + [whole(v) for v in operands],
        out_specs=[whole(o) for o in outs],
        scratch_shapes=list(scratch),
        compiler_params=pltpu.CompilerParams(vmem_limit_bytes=mib * 1024 * 1024),
        name=name,
    )(*(() if numbers is None else (numbers,)), *operands)


def on_device(
    n_z, n_x, node_feats, node_grad, flat_params, rot_table, edge_src, edge_dst, edge_rot,
    edge_owner,
):
    n = edge_src.shape[0]
    cap = n // 4
    width = node_feats.shape[1]
    rows = flat_params.shape[0]
    n_dp = n_z * n_x * 2
    n_rot = rot_table.shape[0]
    z, x, core = (lax.axis_index(a) for a in ALL)
    me = dp_index(n_x)
    smem = pl.BlockSpec(memory_space=pltpu.SMEM)

    def shift(block, step):
        route = [
            (i, i + step) for i in range(n_dp)
            if 0 <= i + step and i // SPAN == (i + step) // SPAN
        ]
        return lax.ppermute(block, ALL, route)

    def swap(block):
        return lax.ppermute(block, "core", [(0, 1), (1, 0)])

    group = lax.axis_index("groups")
    piece = -(-rows // 32) * 16
    part = lax.dynamic_slice_in_dim(flat_params, group * (rows - piece), piece, 0)
    gathered = lax.all_gather(part, ("z", "x"), axis=0)
    crossed = lax.ppermute(gathered, "groups", [(0, 1), (1, 0)])
    weights = [gathered, swap(gathered), crossed, swap(crossed)]

    row = lambda v: v.reshape(1, n)
    here, *outbound = call(
        send_kernel, "send", 60,
        [shape((n // 2, width + 128), BF16)] + [shape((cap, width + 128), BF16)] * 4,
        [row(edge_owner), row(edge_src), row(edge_dst), row(edge_rot), node_feats],
        numbers=me.reshape(1),
    )
    arrived = [shift(r, s) for r, s in zip(outbound, STEPS)]

    tab = rot_table.transpose(1, 0, 2).reshape(K * n_rot, K)
    tabt = rot_table.transpose(2, 0, 1).reshape(K * n_rot, K)

    def rotate(rows_in, name):
        slots = sum(r.shape[0] for r in rows_in)
        return call(
            lambda *refs: rotate_kernel(len(rows_in), *refs), name, 60,
            [
                shape((2 * slots, width), BF16), shape((slots // 8, 240, 256), BF16),
                shape((slots, n), BF16),
            ],
            [*rows_in, tab, tabt, node_grad],
            [
                pltpu.VMEM((slots // 8, 240, 256), BF16), pltpu.VMEM((30, slots, 256), F32),
                pltpu.VMEM((32, slots, 256), F32), pltpu.VMEM((30, slots, 256), F32),
            ],
        )

    both_near, matst_near, hot_near = rotate([here], "rotate_near")
    both_near_other = swap(both_near)
    arrived, both_near, matst_near, hot_near = lax.optimization_barrier(
        (arrived, both_near, matst_near, hot_near)
    )
    both_far, matst_far, hot_far = rotate(arrived, "rotate_far")
    both_far_other = swap(both_far)

    n_send = n_z * (n_x - 1)
    blocks = call(
        lambda *refs: grad_kernel(n_z, n_x, *refs), "weight_terms", 60,
        [shape((rows, 128), BF16)] * n_send + [shape((rows, 128), F32)] * n_z,
        [both_near, both_near_other, both_far, both_far_other],
        [pltpu.VMEM((rows * n_dp, 128), F32)],
        numbers=jnp.stack([z, x, core]),
    )
    arrived = []
    for at, i in enumerate(shifts(n_z)):
        total = blocks[n_send + at]
        for o in range(1, n_x):
            got = lax.ppermute(
                blocks[(o - 1) * n_z + at], "x", [(s, (s + o) % n_x) for s in range(n_x)]
            )
            total = total + got.astype(F32)
        if i:
            term = total.astype(BF16)
            arrived.append(lax.ppermute(term, "z", [(s, (s + i) % n_z) for s in range(n_z)]))
    result = total
    for got in arrived:
        result = result + got.astype(F32)
    weight_grad = result * (1.0 / math.sqrt(n * n_dp))

    weights[3], _ = lax.optimization_barrier((weights[3], term))
    slots = n // 2 + 4 * cap
    (node_out,) = call(
        lambda *refs: message_kernel(rows, *refs), "messages", 60,
        [shape((n, width), BF16)],
        [*weights, both_near, both_far, matst_near, matst_far, hot_near, hot_far],
        [
            pltpu.VMEM((rows * n_dp, 128), F32), pltpu.VMEM((32, slots, 128), F32),
            pltpu.VMEM((30, slots, 128), F32), pltpu.VMEM((slots, width), BF16),
        ],
        numbers=jnp.stack([group, core]),
    )
    return (node_out, weight_grad)


def chips(mesh):
    n_dp = mesh.shape["dp"]
    line = list(mesh.devices.reshape(-1, n_dp)[0])
    coords = [getattr(d, "coords", None) for d in line]
    n_x = 2 if coords[0] is None else len({c[0] for c in coords})
    return n_dp // (2 * n_x), n_x


def solution(mesh):
    n_z, n_x = chips(mesh)
    fine = Mesh(
        np.asarray(mesh.devices).reshape(mesh.shape["groups"], n_z, n_x, 2),
        ("groups", "z", "x", "core"),
    )
    every = ("groups",) + ALL
    placed = (
        P(every, None),
        P(every, None),
        P(ALL, None),
        P(),
        P(every),
        P(every),
        P(every),
        P(every, None),
    )
    return jax.shard_map(
        lambda *args: on_device(n_z, n_x, *args),
        mesh=fine,
        in_specs=placed,
        out_specs=(P(every, None), P(every, None)),
        check_vma=False,
    )
```

```python
import math

import jax
import jax.numpy as jnp
import numpy as np
from jax import lax
from jax.experimental import pallas as pl
from jax.experimental.pallas import tpu as pltpu
from jax.sharding import Mesh, PartitionSpec as P

K = 29
SPAN = 8
STEPS = (-2, -1, 1, 2)
F32 = jnp.float32
BF16 = jnp.bfloat16
ALL = ("z", "x", "core")


def dot(a, b):
    return jnp.dot(a, b, preferred_element_type=F32)


def iota(shape, dim):
    return lax.broadcasted_iota(jnp.int32, shape, dim)


def hot(cond):
    return jnp.where(cond, 1.0, 0.0).astype(BF16)


def column(row):
    n = row.shape[1]
    eye = iota((n, n), 0) == iota((n, n), 1)
    return jnp.sum(jnp.where(eye, row.astype(F32), 0.0), axis=1, keepdims=True)


def dp_index(n_x):
    return (lax.axis_index("z") * n_x + lax.axis_index("x")) * 2 + lax.axis_index("core")


def send_kernel(me_ref, owner_ref, src_ref, dst_ref, rot_ref, feats_ref, *outs):
    n = feats_ref.shape[0]
    width = feats_ref.shape[1]
    half, cap = n // 2, n // 4
    off_row = (owner_ref[...] - me_ref[0]).astype(F32)
    off = column(off_row)
    before = (off == off_row) & (iota((n, n), 0) < iota((n, n), 1))
    slot = jnp.sum(jnp.where(before, 1.0, 0.0), axis=0, keepdims=True)
    for q, step in enumerate(STEPS):
        slot = jnp.where(off_row == step, slot + float(half + q * cap), slot)
    slots = half + 4 * cap
    here = slot == iota((slots, n), 0).astype(F32)

    def pick(row):
        return jnp.sum(jnp.where(here, row, 0.0), axis=1, keepdims=True)

    source = pick(src_ref[...].astype(F32) + 1.0) - 1.0
    target = pick(dst_ref[...].astype(F32) + 1.0)
    turns = pick(rot_ref[...].astype(F32))
    source_hot = hot(source == iota((slots, n), 1).astype(F32))
    lane = iota((slots, 128), 1)
    ids = jnp.where(lane == 0, target, jnp.where(lane == 1, turns, 0.0)).astype(BF16)
    spans = [(0, half)] + [(half + q * cap, cap) for q in range(4)]
    for o, (at, size) in zip(outs, spans):
        o[:, width:] = ids[at : at + size]
    for j, w in chunks():
        cols = slice(j * 128, (j + w) * 128)
        rows = dot(source_hot, feats_ref[:, cols]).astype(BF16)
        for o, (at, size) in zip(outs, spans):
            o[:, cols] = rows[at : at + size]


def turn(mats_ref, src_ref, res_ref):
    lanes = src_ref.shape[2]
    for g in range(src_ref.shape[1] // 8):
        rhs = src_ref[:, 8 * g : 8 * g + 8, :].reshape(256, lanes).astype(BF16)
        res = dot(mats_ref[g], rhs)
        res_ref[:, 8 * g : 8 * g + 8, :] = res.reshape(30, 8, lanes)


def build(table_ref, rot_hot, mats_ref, tmp_ref):
    n = rot_hot.shape[0]
    n_rot = rot_hot.shape[1]
    spread = hot(iota((K, 256), 1) // 8 == iota((K, 256), 0))
    wide = dot(table_ref[...], spread).astype(BF16)
    own = (iota((n, 256), 1) % 8) == (iota((n, 256), 0) % 8)
    for k in range(K):
        tmp_ref[k] = jnp.where(own, dot(rot_hot, wide[k * n_rot : (k + 1) * n_rot]), 0.0)
    tmp_ref[K] = jnp.zeros((n, 256), F32)
    for g in range(n // 8):
        mats_ref[g] = tmp_ref[:, 8 * g : 8 * g + 8, :].reshape(240, 256).astype(BF16)


def chunks():
    j = 0
    while j < K:
        w = min(4, K - j)
        yield j, w
        j += w


def joined(refs, cols):
    return jnp.concatenate([r[:, cols] for r in refs], axis=0)


def number(ids, lane):
    at = iota(ids.shape, 1) == lane
    return jnp.sum(jnp.where(at, ids.astype(F32), 0.0), axis=1, keepdims=True)


def rotate_kernel(count, *refs):
    raw, (tab_ref, grad_ref) = refs[:count], refs[count : count + 2]
    both_ref, hot_ref, turn_ref, mats_ref, tmp_ref, in_ref, res_ref = refs[count + 2 :]
    n = grad_ref.shape[0]
    n_rot = tab_ref.shape[0] // K
    width = grad_ref.shape[1]
    ids = joined(raw, slice(width, width + 128))
    slots = ids.shape[0]
    target_hot = hot(number(ids, 0) - 1.0 == iota((slots, n), 1).astype(F32))
    rot_hot = hot(number(ids, 1) == iota((slots, n_rot), 1).astype(F32))
    hot_ref[...] = target_hot
    turn_ref[...] = rot_hot
    for j, w in chunks():
        cols = slice(j * 128, (j + w) * 128)
        rows = joined(raw, cols).astype(F32)
        back = dot(target_hot, grad_ref[:, cols])
        for i in range(w):
            in_ref[j + i, :, :128] = rows[:, 128 * i : 128 * i + 128]
            in_ref[j + i, :, 128:] = back[:, 128 * i : 128 * i + 128]
    for j in range(K, 32):
        in_ref[j] = jnp.zeros((slots, 256), F32)
    build(tab_ref, rot_hot, mats_ref, tmp_ref)
    turn(mats_ref, in_ref, res_ref)
    for k in range(K):
        cols = slice(k * 128, (k + 1) * 128)
        both_ref[:slots, cols] = res_ref[k, :, :128].astype(BF16)
        both_ref[slots:, cols] = res_ref[k, :, 128:].astype(BF16)


def back_kernel(near_ref, far_ref, tabt_ref, near_out, far_out, near_tmp, far_tmp):
    build(tabt_ref, near_ref[...], near_out, near_tmp)
    build(tabt_ref, far_ref[...], far_out, far_tmp)


def shifts(n_z):
    return sorted(range(n_z), key=lambda i: (i == 0, abs(i - n_z // 2)))


def grad_kernel(n_z, n_x, pos_ref, *refs):
    parts, outs, flat = refs[:4], refs[4:-1], refs[-1]
    z, x, core = pos_ref[0], pos_ref[1], pos_ref[2]

    def left(first, width):
        at = slice(first * 128, (first + width) * 128)
        return [p[: p.shape[0] // 2, at] for p in parts]

    def right(first, width):
        at = slice(first * 128, (first + width) * 128)
        return [p[p.shape[0] // 2 :, at] for p in parts]

    def outer(lhs, rhs):
        return lax.dot_general(lhs, rhs, (((0,), (0,)), ((), ())), preferred_element_type=F32)

    def emit(base, width, res):
        for b in range(width):
            flat[pl.ds(base + b, width * 128, stride=width), :] = res[:, b * 128 : (b + 1) * 128]

    emit(0, 7, outer(jnp.concatenate(left(0, 7), axis=0), jnp.concatenate(right(0, 7), axis=0)))
    base = 49 * 128
    for first, width in ((7, 6), (19, 5)):
        lhs = jnp.concatenate(left(first, width) + left(first + width, width), axis=0)
        real, imag = right(first, width), right(first + width, width)
        emit(base, width, outer(lhs, jnp.concatenate(real + imag, axis=0)))
        base += width * width * 128
        emit(base, width, outer(lhs, jnp.concatenate(imag + [-v for v in real], axis=0)))
        base += width * width * 128

    rows = outs[0].shape[0]
    at_out = 0
    for o in list(range(1, n_x)) + [0]:
        for i in shifts(n_z):
            start = (((z + i) % n_z * n_x + (x + o) % n_x) * 2 + core) * rows
            if rows % 8 == 0:
                start = pl.multiple_of(start, 8)
            ref = outs[at_out]
            ref[...] = flat[pl.ds(start, rows), :].astype(ref.dtype)
            at_out += 1


def message_kernel(w_ref, *refs):
    both, mats, hots = refs[0:2], refs[2:4], refs[4:6]
    out_ref, flat, in_ref, res_ref, wide_ref = refs[6:]
    n = out_ref.shape[0]
    slots = in_ref.shape[1]
    part = w_ref.shape[0] // 16
    for p in range(16):
        flat[p * part : (p + 1) * part, :] = w_ref[p * part : (p + 1) * part, :].astype(F32)

    def h(first, end):
        return jnp.concatenate(
            [r[: r.shape[0] // 2, first * 128 : end * 128] for r in both], axis=0
        )

    def fill(j, wide):
        for i in range(wide.shape[1] // 128):
            in_ref[j + i] = wide[:, 128 * i : 128 * i + 128]

    def weight(base, width, b, many):
        parts = [
            flat[pl.ds(base + b + t, width * 128, stride=width), :].astype(BF16)
            for t in range(many)
        ]
        return parts[0] if many == 1 else jnp.concatenate(parts, axis=1)

    def rounded(v):
        return v.astype(BF16).astype(F32)

    def pairs(width):
        return [(b, min(2, width - b)) for b in range(0, width, 2)]

    h0 = h(0, 7)
    for b, many in pairs(7):
        fill(b, rounded(dot(h0, weight(0, 7, b, many))))
    base = 49 * 128
    for first, width in ((7, 6), (19, 5)):
        mid, end = first + width, first + 2 * width
        pair = jnp.concatenate([h(first, mid), h(mid, end)], axis=0)
        for b, many in pairs(width):
            real = dot(pair, weight(base, width, b, many))
            imag = dot(pair, weight(base + width * width * 128, width, b, many))
            fill(first + b, rounded(real[:slots] - imag[slots:]))
            fill(mid + b, rounded(imag[:slots] + real[slots:]))
        base += 2 * width * width * 128
    for j in range(K, 32):
        in_ref[j] = jnp.zeros((slots, 128), F32)
    at = 0
    for m in mats:
        size = m.shape[0] * 8
        turn(m, in_ref.at[:, at : at + size, :], res_ref.at[:, at : at + size, :])
        at += size
    for k in range(K):
        wide_ref[:, k * 128 : (k + 1) * 128] = res_ref[k].astype(BF16)
    target = jnp.concatenate([r[...] for r in hots], axis=0).astype(F32).T.astype(BF16)
    for j, w in chunks():
        cols = slice(j * 128, (j + w) * 128)
        out_ref[:, cols] = dot(target, wide_ref[:, cols]).astype(BF16)


def shape(dims, kind):
    return jax.ShapeDtypeStruct(dims, kind)


def whole(like):
    zeros = (0,) * len(like.shape)
    return pl.BlockSpec(like.shape, lambda i: zeros, pipeline_mode=pl.Buffered(1))


def call(kernel, name, mib, outs, operands, scratch=(), numbers=None):
    first = [] if numbers is None else [pl.BlockSpec(memory_space=pltpu.SMEM)]
    return pl.pallas_call(
        kernel,
        grid=(1,),
        out_shape=outs,
        in_specs=first + [whole(v) for v in operands],
        out_specs=[whole(o) for o in outs],
        scratch_shapes=list(scratch),
        compiler_params=pltpu.CompilerParams(vmem_limit_bytes=mib * 1024 * 1024),
        name=name,
    )(*(() if numbers is None else (numbers,)), *operands)


def on_device(
    n_z, n_x, node_feats, node_grad, flat_params, rot_table, edge_src, edge_dst, edge_rot,
    edge_owner,
):
    n = edge_src.shape[0]
    cap = n // 4
    width = node_feats.shape[1]
    rows = flat_params.shape[0]
    n_dp = n_z * n_x * 2
    n_rot = rot_table.shape[0]
    z, x, core = (lax.axis_index(a) for a in ALL)
    me = dp_index(n_x)
    smem = pl.BlockSpec(memory_space=pltpu.SMEM)

    def shift(block, step):
        route = [
            (i, i + step) for i in range(n_dp)
            if 0 <= i + step and i // SPAN == (i + step) // SPAN
        ]
        return lax.ppermute(block, ALL, route)

    def swap(block):
        return lax.ppermute(block, "core", [(0, 1), (1, 0)])

    weights = lax.all_gather(flat_params, ALL, axis=0, tiled=True)

    row = lambda v: v.reshape(1, n)
    here, *outbound = call(
        send_kernel, "send", 60,
        [shape((n // 2, width + 128), BF16)] + [shape((cap, width + 128), BF16)] * 4,
        [row(edge_owner), row(edge_src), row(edge_dst), row(edge_rot), node_feats],
        numbers=me.reshape(1),
    )
    arrived = [shift(r, s) for r, s in zip(outbound, STEPS)]

    tab = rot_table.transpose(1, 0, 2).reshape(K * n_rot, K)
    tabt = rot_table.transpose(2, 0, 1).reshape(K * n_rot, K)

    def rotate(rows_in, name):
        slots = sum(r.shape[0] for r in rows_in)
        return call(
            lambda *refs: rotate_kernel(len(rows_in), *refs), name, 60,
            [
                shape((2 * slots, width), BF16), shape((slots, n), BF16),
                shape((slots, n_rot), BF16),
            ],
            [*rows_in, tab, node_grad],
            [
                pltpu.VMEM((slots // 8, 240, 256), BF16), pltpu.VMEM((30, slots, 256), F32),
                pltpu.VMEM((32, slots, 256), F32), pltpu.VMEM((30, slots, 256), F32),
            ],
        )

    both_near, hot_near, turn_near = rotate([here], "rotate_near")
    both_near_other = swap(both_near)
    arrived, both_near = lax.optimization_barrier((arrived, both_near))
    both_far, hot_far, turn_far = rotate(arrived, "rotate_far")
    both_far_other = swap(both_far)

    n_send = n_z * (n_x - 1)
    blocks = call(
        lambda *refs: grad_kernel(n_z, n_x, *refs), "weight_terms", 60,
        [shape((rows, 128), BF16)] * n_send + [shape((rows, 128), F32)] * n_z,
        [both_near, both_near_other, both_far, both_far_other],
        [pltpu.VMEM((rows * n_dp, 128), F32)],
        numbers=jnp.stack([z, x, core]),
    )
    turn_far, blocks = lax.optimization_barrier((turn_far, blocks))
    matst_near, matst_far = call(
        back_kernel, "back", 60,
        [shape((t.shape[0] // 8, 240, 256), BF16) for t in (turn_near, turn_far)],
        [turn_near, turn_far, tabt],
        [pltpu.VMEM((30, t.shape[0], 256), F32) for t in (turn_near, turn_far)],
    )
    arrived, terms = [], []
    for at, i in enumerate(shifts(n_z)):
        total = blocks[n_send + at]
        for o in range(1, n_x):
            got = lax.ppermute(
                blocks[(o - 1) * n_z + at], "x", [(s, (s + o) % n_x) for s in range(n_x)]
            )
            total = total + got.astype(F32)
        if i:
            terms.append(total.astype(BF16))
            arrived.append(lax.ppermute(terms[-1], "z", [(s, (s + i) % n_z) for s in range(n_z)]))
    weights, _ = lax.optimization_barrier((weights, terms[-1]))
    slots = n // 2 + 4 * cap
    (node_out,) = call(
        message_kernel, "messages", 60,
        [shape((n, width), BF16)],
        [weights, both_near, both_far, matst_near, matst_far, hot_near, hot_far],
        [
            pltpu.VMEM((rows * n_dp, 128), F32), pltpu.VMEM((32, slots, 128), F32),
            pltpu.VMEM((30, slots, 128), F32), pltpu.VMEM((slots, width), BF16),
        ],
    )
    arrived[-1], node_out = lax.optimization_barrier((arrived[-1], node_out))
    result = total
    for got in arrived:
        result = result + got.astype(F32)
    weight_grad = result * (1.0 / math.sqrt(n * n_dp))
    return (node_out, weight_grad)


def chips(mesh):
    n_dp = mesh.shape["dp"]
    line = list(mesh.devices.reshape(-1, n_dp)[0])
    coords = [getattr(d, "coords", None) for d in line]
    n_x = 2 if coords[0] is None else len({c[0] for c in coords})
    return n_dp // (2 * n_x), n_x


def solution(mesh):
    n_z, n_x = chips(mesh)
    fine = Mesh(
        np.asarray(mesh.devices).reshape(mesh.shape["groups"], n_z, n_x, 2),
        ("groups", "z", "x", "core"),
    )
    every = ("groups",) + ALL
    placed = (
        P(every, None),
        P(every, None),
        P(ALL, None),
        P(),
        P(every),
        P(every),
        P(every),
        P(every, None),
    )
    return jax.shard_map(
        lambda *args: on_device(n_z, n_x, *args),
        mesh=fine,
        in_specs=placed,
        out_specs=(P(every, None), P(every, None)),
        check_vma=False,
    )
```

```python
import math

import jax
import jax.numpy as jnp
import numpy as np
from jax import lax
from jax.experimental import pallas as pl
from jax.experimental.pallas import tpu as pltpu
from jax.sharding import Mesh, PartitionSpec as P

K = 29
SPAN = 8
STEPS = (-2, 2, -1, 1)
F32 = jnp.float32
BF16 = jnp.bfloat16
ALL = ("z", "x", "core")


def dot(a, b):
    return jnp.dot(a, b, preferred_element_type=F32)


def iota(shape, dim):
    return lax.broadcasted_iota(jnp.int32, shape, dim)


def hot(cond):
    return jnp.where(cond, 1.0, 0.0).astype(BF16)


def column(row):
    n = row.shape[1]
    eye = iota((n, n), 0) == iota((n, n), 1)
    return jnp.sum(jnp.where(eye, row.astype(F32), 0.0), axis=1, keepdims=True)


def dp_index(n_x):
    return (lax.axis_index("z") * n_x + lax.axis_index("x")) * 2 + lax.axis_index("core")


def send_kernel(me_ref, owner_ref, src_ref, dst_ref, rot_ref, feats_ref, *outs):
    n = feats_ref.shape[0]
    width = feats_ref.shape[1]
    half, cap = n // 2, n // 4
    off_row = (owner_ref[...] - me_ref[0]).astype(F32)
    off = column(off_row)
    before = (off == off_row) & (iota((n, n), 0) < iota((n, n), 1))
    slot = jnp.sum(jnp.where(before, 1.0, 0.0), axis=0, keepdims=True)
    for q, step in enumerate(STEPS):
        slot = jnp.where(off_row == step, slot + float(half + q * cap), slot)
    slots = half + 4 * cap
    here = slot == iota((slots, n), 0).astype(F32)

    def pick(row):
        return jnp.sum(jnp.where(here, row, 0.0), axis=1, keepdims=True)

    source = pick(src_ref[...].astype(F32) + 1.0) - 1.0
    target = pick(dst_ref[...].astype(F32) + 1.0)
    turns = pick(rot_ref[...].astype(F32))
    source_hot = hot(source == iota((slots, n), 1).astype(F32))
    lane = iota((slots, 128), 1)
    ids = jnp.where(lane == 0, target, jnp.where(lane == 1, turns, 0.0)).astype(BF16)
    spans = [(0, half)] + [(half + q * cap, cap) for q in range(4)]
    for o, (at, size) in zip(outs, spans):
        o[:, width:] = ids[at : at + size]
    for j, w in chunks():
        cols = slice(j * 128, (j + w) * 128)
        rows = dot(source_hot, feats_ref[:, cols]).astype(BF16)
        for o, (at, size) in zip(outs, spans):
            o[:, cols] = rows[at : at + size]


def turn(mats_ref, src_ref, res_ref):
    lanes = src_ref.shape[2]
    for g in range(src_ref.shape[1] // 8):
        rhs = src_ref[:, 8 * g : 8 * g + 8, :].reshape(256, lanes).astype(BF16)
        res = dot(mats_ref[g], rhs)
        res_ref[:, 8 * g : 8 * g + 8, :] = res.reshape(30, 8, lanes)


def build(table_ref, rot_hot, mats_ref, tmp_ref):
    n = rot_hot.shape[0]
    n_rot = rot_hot.shape[1]
    spread = hot(iota((K, 256), 1) // 8 == iota((K, 256), 0))
    wide = dot(table_ref[...], spread).astype(BF16)
    own = (iota((n, 256), 1) % 8) == (iota((n, 256), 0) % 8)
    for k in range(K):
        tmp_ref[k] = jnp.where(own, dot(rot_hot, wide[k * n_rot : (k + 1) * n_rot]), 0.0)
    tmp_ref[K] = jnp.zeros((n, 256), F32)
    for g in range(n // 8):
        mats_ref[g] = tmp_ref[:, 8 * g : 8 * g + 8, :].reshape(240, 256).astype(BF16)


def chunks():
    j = 0
    while j < K:
        w = min(4, K - j)
        yield j, w
        j += w


def joined(refs, cols):
    return jnp.concatenate([r[:, cols] for r in refs], axis=0)


def number(ids, lane):
    at = iota(ids.shape, 1) == lane
    return jnp.sum(jnp.where(at, ids.astype(F32), 0.0), axis=1, keepdims=True)


def rotate_kernel(count, *refs):
    raw, (tab_ref, grad_ref) = refs[:count], refs[count : count + 2]
    both_ref, hot_ref, turn_ref, mats_ref, tmp_ref, in_ref, res_ref = refs[count + 2 :]
    n = grad_ref.shape[0]
    n_rot = tab_ref.shape[0] // K
    width = grad_ref.shape[1]
    ids = joined(raw, slice(width, width + 128))
    slots = ids.shape[0]
    target_hot = hot(number(ids, 0) - 1.0 == iota((slots, n), 1).astype(F32))
    rot_hot = hot(number(ids, 1) == iota((slots, n_rot), 1).astype(F32))
    hot_ref[...] = target_hot
    turn_ref[...] = rot_hot
    for j, w in chunks():
        cols = slice(j * 128, (j + w) * 128)
        rows = joined(raw, cols).astype(F32)
        back = dot(target_hot, grad_ref[:, cols])
        for i in range(w):
            in_ref[j + i, :, :128] = rows[:, 128 * i : 128 * i + 128]
            in_ref[j + i, :, 128:] = back[:, 128 * i : 128 * i + 128]
    for j in range(K, 32):
        in_ref[j] = jnp.zeros((slots, 256), F32)
    build(tab_ref, rot_hot, mats_ref, tmp_ref)
    turn(mats_ref, in_ref, res_ref)
    for k in range(K):
        cols = slice(k * 128, (k + 1) * 128)
        both_ref[:slots, cols] = res_ref[k, :, :128].astype(BF16)
        both_ref[slots:, cols] = res_ref[k, :, 128:].astype(BF16)


def back_kernel(tabt_ref, *refs):
    for i in range(2):
        build(tabt_ref, refs[i][...], refs[2 + i], refs[4 + i])


def shifts(n_z):
    return sorted(range(n_z), key=lambda i: (i == 0, abs(i - n_z // 2)))


def grad_kernel(n_z, n_x, me_ref, *refs):
    parts, outs, flat = refs[:4], refs[4:-1], refs[-1]
    chip, core = me_ref[0] // 2, me_ref[0] % 2
    z, x = chip // n_x, chip % n_x

    def left(first, width):
        at = slice(first * 128, (first + width) * 128)
        return [p[: p.shape[0] // 2, at] for p in parts]

    def right(first, width):
        at = slice(first * 128, (first + width) * 128)
        return [p[p.shape[0] // 2 :, at] for p in parts]

    def outer(lhs, rhs):
        return lax.dot_general(lhs, rhs, (((0,), (0,)), ((), ())), preferred_element_type=F32)

    def emit(base, width, res):
        for b in range(width):
            flat[pl.ds(base + b, width * 128, stride=width), :] = res[:, b * 128 : (b + 1) * 128]

    emit(0, 7, outer(jnp.concatenate(left(0, 7), axis=0), jnp.concatenate(right(0, 7), axis=0)))
    base = 49 * 128
    for first, width in ((7, 6), (19, 5)):
        lhs = jnp.concatenate(left(first, width) + left(first + width, width), axis=0)
        real, imag = right(first, width), right(first + width, width)
        emit(base, width, outer(lhs, jnp.concatenate(real + imag, axis=0)))
        base += width * width * 128
        emit(base, width, outer(lhs, jnp.concatenate(imag + [-v for v in real], axis=0)))
        base += width * width * 128

    rows = outs[0].shape[0]
    at_out = 0
    for o in list(range(1, n_x)) + [0]:
        for i in shifts(n_z):
            start = (((z + i) % n_z * n_x + (x + o) % n_x) * 2 + core) * rows
            if rows % 8 == 0:
                start = pl.multiple_of(start, 8)
            ref = outs[at_out]
            ref[...] = flat[pl.ds(start, rows), :].astype(ref.dtype)
            at_out += 1


def message_kernel(w_ref, *refs):
    both, mats, hots = refs[0:2], refs[2:4], refs[4:6]
    out_ref, flat, in_ref, res_ref, wide_ref = refs[6:]
    n = out_ref.shape[0]
    slots = in_ref.shape[1]
    part = w_ref.shape[0] // 16
    for p in range(16):
        flat[p * part : (p + 1) * part, :] = w_ref[p * part : (p + 1) * part, :].astype(F32)

    def h(first, end):
        return jnp.concatenate(
            [r[: r.shape[0] // 2, first * 128 : end * 128] for r in both], axis=0
        )

    def fill(j, wide):
        for i in range(wide.shape[1] // 128):
            in_ref[j + i] = wide[:, 128 * i : 128 * i + 128]

    def weight(base, width, b, many):
        parts = [
            flat[pl.ds(base + b + t, width * 128, stride=width), :].astype(BF16)
            for t in range(many)
        ]
        return parts[0] if many == 1 else jnp.concatenate(parts, axis=1)

    def rounded(v):
        return v.astype(BF16).astype(F32)

    def pairs(width):
        return [(b, min(2, width - b)) for b in range(0, width, 2)]

    h0 = h(0, 7)
    for b, many in pairs(7):
        fill(b, rounded(dot(h0, weight(0, 7, b, many))))
    base = 49 * 128
    for first, width in ((7, 6), (19, 5)):
        mid, end = first + width, first + 2 * width
        pair = jnp.concatenate([h(first, mid), h(mid, end)], axis=0)
        for b, many in pairs(width):
            real = dot(pair, weight(base, width, b, many))
            imag = dot(pair, weight(base + width * width * 128, width, b, many))
            fill(first + b, rounded(real[:slots] - imag[slots:]))
            fill(mid + b, rounded(imag[:slots] + real[slots:]))
        base += 2 * width * width * 128
    for j in range(K, 32):
        in_ref[j] = jnp.zeros((slots, 128), F32)
    at = 0
    for m in mats:
        size = m.shape[0] * 8
        turn(m, in_ref.at[:, at : at + size, :], res_ref.at[:, at : at + size, :])
        at += size
    for k in range(K):
        wide_ref[:, k * 128 : (k + 1) * 128] = res_ref[k].astype(BF16)
    target = jnp.concatenate([r[...] for r in hots], axis=0).astype(F32).T.astype(BF16)
    for j, w in chunks():
        cols = slice(j * 128, (j + w) * 128)
        out_ref[:, cols] = dot(target, wide_ref[:, cols]).astype(BF16)


def shape(dims, kind):
    return jax.ShapeDtypeStruct(dims, kind)


def whole(like):
    zeros = (0,) * len(like.shape)
    return pl.BlockSpec(like.shape, lambda i: zeros, pipeline_mode=pl.Buffered(1))


def call(kernel, name, mib, outs, operands, scratch=(), numbers=None, cost=None):
    first = [] if numbers is None else [pl.BlockSpec(memory_space=pltpu.SMEM)]
    return pl.pallas_call(
        kernel,
        grid=(1,),
        out_shape=outs,
        in_specs=first + [whole(v) for v in operands],
        out_specs=[whole(o) for o in outs],
        scratch_shapes=list(scratch),
        compiler_params=pltpu.CompilerParams(vmem_limit_bytes=mib * 1024 * 1024),
        cost_estimate=cost,
        name=name,
    )(*(() if numbers is None else (numbers,)), *operands)


def on_device(
    n_z, n_x, node_feats, node_grad, flat_params, rot_table, edge_src, edge_dst, edge_rot,
    edge_owner,
):
    n = edge_src.shape[0]
    cap = n // 4
    width = node_feats.shape[1]
    rows = flat_params.shape[0]
    n_dp = n_z * n_x * 2
    n_rot = rot_table.shape[0]
    me = dp_index(n_x)
    smem = pl.BlockSpec(memory_space=pltpu.SMEM)

    def shift(block, step):
        route = [
            (i, i + step) for i in range(n_dp)
            if 0 <= i + step and i // SPAN == (i + step) // SPAN
        ]
        return lax.ppermute(block, ALL, route)

    def swap(block):
        return lax.ppermute(block, "core", [(0, 1), (1, 0)])

    weights = lax.all_gather(flat_params, ALL, axis=0, tiled=True)

    row = lambda v: v.reshape(1, n)
    here, *outbound = call(
        send_kernel, "send", 62,
        [shape((n // 2, width + 128), BF16)] + [shape((cap, width + 128), BF16)] * 4,
        [row(edge_owner), row(edge_src), row(edge_dst), row(edge_rot), node_feats],
        numbers=me.reshape(1),
    )
    arrived = [shift(r, s) for r, s in zip(outbound, STEPS)]

    tab = rot_table.transpose(1, 0, 2).reshape(K * n_rot, K)
    tabt = rot_table.transpose(2, 0, 1).reshape(K * n_rot, K)

    def rotate(rows_in, name, cost=None):
        slots = sum(r.shape[0] for r in rows_in)
        return call(
            lambda *refs: rotate_kernel(len(rows_in), *refs), name, 62,
            [
                shape((2 * slots, width), BF16), shape((slots, n), BF16),
                shape((slots, n_rot), BF16),
            ],
            [*rows_in, tab, node_grad],
            [
                pltpu.VMEM((slots // 8, 240, 256), BF16), pltpu.VMEM((30, slots, 256), F32),
                pltpu.VMEM((32, slots, 256), F32), pltpu.VMEM((30, slots, 256), F32),
            ],
            cost=cost,
        )

    both_a, hot_a, turn_a = rotate([here] + arrived[:2], "rotate_first")
    both_a_other = swap(both_a)
    last, both_a = lax.optimization_barrier((arrived[2:], both_a))
    both_b, hot_b, turn_b = rotate(
        last, "rotate_last",
        pl.CostEstimate(flops=10**10, bytes_accessed=10**8, transcendentals=0),
    )
    both_b_other = swap(both_b)
    both, hots, turns = [both_a, both_b], [hot_a, hot_b], [turn_a, turn_b]

    n_send = n_z * (n_x - 1)
    blocks = call(
        lambda *refs: grad_kernel(n_z, n_x, *refs), "weight_terms", 62,
        [shape((rows, 128), BF16)] * n_send + [shape((rows, 128), F32)] * n_z,
        both + [both_a_other, both_b_other],
        [pltpu.VMEM((rows * n_dp, 128), F32)],
        numbers=me.reshape(1),
    )
    turns, blocks = lax.optimization_barrier((turns, list(blocks)))
    mats = call(
        back_kernel, "back", 62,
        [shape((t.shape[0] // 8, 240, 256), BF16) for t in turns],
        [tabt] + turns,
        [pltpu.VMEM((30, t.shape[0], 256), F32) for t in turns],
    )
    kept = blocks[n_send:]
    kept[0], mats = lax.optimization_barrier((kept[0], mats))
    arrived, terms = [], []
    for at, i in enumerate(shifts(n_z)):
        total = kept[at]
        if at == 2:
            weights, _ = lax.optimization_barrier((weights, terms[1]))
            slots = n // 2 + 4 * cap
            (node_out,) = call(
                message_kernel, "messages", 62,
                [shape((n, width), BF16)],
                [weights, *both, *mats, *hots],
                [
                    pltpu.VMEM((rows * n_dp, 128), F32), pltpu.VMEM((32, slots, 128), F32),
                    pltpu.VMEM((30, slots, 128), F32), pltpu.VMEM((slots, width), BF16),
                ],
            )
            total, node_out = lax.optimization_barrier((total, node_out))
        for o in range(1, n_x):
            got = lax.ppermute(
                blocks[(o - 1) * n_z + at], "x", [(s, (s + o) % n_x) for s in range(n_x)]
            )
            total = total + got.astype(F32)
        if i:
            terms.append(total.astype(BF16))
            arrived.append(lax.ppermute(terms[-1], "z", [(s, (s + i) % n_z) for s in range(n_z)]))
    result = total
    for got in arrived:
        result = result + got.astype(F32)
    weight_grad = result * (1.0 / math.sqrt(n * n_dp))
    return (node_out, weight_grad)


def chips(mesh):
    n_dp = mesh.shape["dp"]
    line = list(mesh.devices.reshape(-1, n_dp)[0])
    coords = [getattr(d, "coords", None) for d in line]
    n_x = 2 if coords[0] is None else len({c[0] for c in coords})
    return n_dp // (2 * n_x), n_x


def solution(mesh):
    n_z, n_x = chips(mesh)
    fine = Mesh(
        np.asarray(mesh.devices).reshape(mesh.shape["groups"], n_z, n_x, 2),
        ("groups", "z", "x", "core"),
    )
    every = ("groups",) + ALL
    placed = (
        P(every, None),
        P(every, None),
        P(ALL, None),
        P(),
        P(every),
        P(every),
        P(every),
        P(every, None),
    )
    return jax.shard_map(
        lambda *args: on_device(n_z, n_x, *args),
        mesh=fine,
        in_specs=placed,
        out_specs=(P(every, None), P(every, None)),
        check_vma=False,
    )
```

```python
import math

import jax
import jax.numpy as jnp
import numpy as np
from jax import lax
from jax.experimental import pallas as pl
from jax.experimental.pallas import tpu as pltpu
from jax.sharding import Mesh, PartitionSpec as P

K = 29
SPAN = 8
STEPS = (-2, 2, -1, 1)
F32 = jnp.float32
BF16 = jnp.bfloat16
ALL = ("z", "x", "core")


def dot(a, b):
    return jnp.dot(a, b, preferred_element_type=F32)


def iota(shape, dim):
    return lax.broadcasted_iota(jnp.int32, shape, dim)


def hot(cond):
    return jnp.where(cond, 1.0, 0.0).astype(BF16)


def column(row):
    n = row.shape[1]
    eye = iota((n, n), 0) == iota((n, n), 1)
    return jnp.sum(jnp.where(eye, row.astype(F32), 0.0), axis=1, keepdims=True)


def dp_index(n_x):
    return (lax.axis_index("z") * n_x + lax.axis_index("x")) * 2 + lax.axis_index("core")


def send_kernel(me_ref, owner_ref, src_ref, dst_ref, rot_ref, feats_ref, *outs):
    n = feats_ref.shape[0]
    width = feats_ref.shape[1]
    half, cap = n // 2, n // 4
    off_row = (owner_ref[...] - me_ref[0]).astype(F32)
    off = column(off_row)
    before = (off == off_row) & (iota((n, n), 0) < iota((n, n), 1))
    slot = jnp.sum(jnp.where(before, 1.0, 0.0), axis=0, keepdims=True)
    for q, step in enumerate(STEPS):
        slot = jnp.where(off_row == step, slot + float(half + q * cap), slot)
    slots = half + 4 * cap
    here = slot == iota((slots, n), 0).astype(F32)

    def pick(row):
        return jnp.sum(jnp.where(here, row, 0.0), axis=1, keepdims=True)

    source = pick(src_ref[...].astype(F32) + 1.0) - 1.0
    target = pick(dst_ref[...].astype(F32) + 1.0)
    turns = pick(rot_ref[...].astype(F32))
    source_hot = hot(source == iota((slots, n), 1).astype(F32))
    lane = iota((slots, 128), 1)
    ids = jnp.where(lane == 0, target, jnp.where(lane == 1, turns, 0.0)).astype(BF16)
    spans = [(0, half)] + [(half + q * cap, cap) for q in range(4)]
    for o, (at, size) in zip(outs, spans):
        o[:, width:] = ids[at : at + size]
    for j, w in chunks():
        cols = slice(j * 128, (j + w) * 128)
        rows = dot(source_hot, feats_ref[:, cols]).astype(BF16)
        for o, (at, size) in zip(outs, spans):
            o[:, cols] = rows[at : at + size]


def turn(mats_ref, src_ref, res_ref):
    lanes = src_ref.shape[2]
    for g in range(src_ref.shape[1] // 8):
        rhs = src_ref[:, 8 * g : 8 * g + 8, :].reshape(256, lanes).astype(BF16)
        res = dot(mats_ref[g], rhs)
        res_ref[:, 8 * g : 8 * g + 8, :] = res.reshape(30, 8, lanes)


def build(table_ref, rot_hot, mats_ref, tmp_ref):
    n = rot_hot.shape[0]
    n_rot = rot_hot.shape[1]
    spread = hot(iota((K, 256), 1) // 8 == iota((K, 256), 0))
    wide = dot(table_ref[...], spread).astype(BF16)
    own = (iota((n, 256), 1) % 8) == (iota((n, 256), 0) % 8)
    for k in range(K):
        tmp_ref[k] = jnp.where(own, dot(rot_hot, wide[k * n_rot : (k + 1) * n_rot]), 0.0)
    tmp_ref[K] = jnp.zeros((n, 256), F32)
    for g in range(n // 8):
        mats_ref[g] = tmp_ref[:, 8 * g : 8 * g + 8, :].reshape(240, 256).astype(BF16)


def chunks():
    j = 0
    while j < K:
        w = min(4, K - j)
        yield j, w
        j += w


def joined(refs, cols):
    return jnp.concatenate([r[:, cols] for r in refs], axis=0)


def number(ids, lane):
    at = iota(ids.shape, 1) == lane
    return jnp.sum(jnp.where(at, ids.astype(F32), 0.0), axis=1, keepdims=True)


def rotate_kernel(count, *refs):
    raw, (tab_ref, grad_ref) = refs[:count], refs[count : count + 2]
    both_ref, hot_ref, turn_ref, mats_ref, tmp_ref, in_ref, res_ref = refs[count + 2 :]
    n = grad_ref.shape[0]
    n_rot = tab_ref.shape[0] // K
    width = grad_ref.shape[1]
    ids = joined(raw, slice(width, width + 128))
    slots = ids.shape[0]
    target_hot = hot(number(ids, 0) - 1.0 == iota((slots, n), 1).astype(F32))
    rot_hot = hot(number(ids, 1) == iota((slots, n_rot), 1).astype(F32))
    hot_ref[...] = target_hot
    turn_ref[...] = rot_hot
    for j, w in chunks():
        cols = slice(j * 128, (j + w) * 128)
        rows = joined(raw, cols).astype(F32)
        back = dot(target_hot, grad_ref[:, cols])
        for i in range(w):
            in_ref[j + i, :, :128] = rows[:, 128 * i : 128 * i + 128]
            in_ref[j + i, :, 128:] = back[:, 128 * i : 128 * i + 128]
    for j in range(K, 32):
        in_ref[j] = jnp.zeros((slots, 256), F32)
    build(tab_ref, rot_hot, mats_ref, tmp_ref)
    turn(mats_ref, in_ref, res_ref)
    for k in range(K):
        cols = slice(k * 128, (k + 1) * 128)
        both_ref[:slots, cols] = res_ref[k, :, :128].astype(BF16)
        both_ref[slots:, cols] = res_ref[k, :, 128:].astype(BF16)


def back_kernel(tabt_ref, *refs):
    for i in range(2):
        build(tabt_ref, refs[i][...], refs[2 + i], refs[4 + i])


def grad_kernel(n_z, n_x, me_ref, *refs):
    parts, outs, flat = refs[:4], refs[4:-1], refs[-1]
    chip, core = me_ref[0] // 2, me_ref[0] % 2
    z, x = chip // n_x, chip % n_x

    def left(first, width):
        at = slice(first * 128, (first + width) * 128)
        return [p[: p.shape[0] // 2, at] for p in parts]

    def right(first, width):
        at = slice(first * 128, (first + width) * 128)
        return [p[p.shape[0] // 2 :, at] for p in parts]

    def outer(lhs, rhs):
        return lax.dot_general(lhs, rhs, (((0,), (0,)), ((), ())), preferred_element_type=F32)

    def emit(base, width, res):
        for b in range(width):
            flat[pl.ds(base + b, width * 128, stride=width), :] = res[:, b * 128 : (b + 1) * 128]

    emit(0, 7, outer(jnp.concatenate(left(0, 7), axis=0), jnp.concatenate(right(0, 7), axis=0)))
    base = 49 * 128
    for first, width in ((7, 6), (19, 5)):
        lhs = jnp.concatenate(left(first, width) + left(first + width, width), axis=0)
        real, imag = right(first, width), right(first + width, width)
        emit(base, width, outer(lhs, jnp.concatenate(real + imag, axis=0)))
        base += width * width * 128
        emit(base, width, outer(lhs, jnp.concatenate(imag + [-v for v in real], axis=0)))
        base += width * width * 128

    rows = outs[0].shape[0]
    at_out = 0
    for o in list(range(1, n_x)) + [0]:
        for r in reversed(range(n_z)):
            start = (((z ^ r) * n_x + (x + o) % n_x) * 2 + core) * rows
            if rows % 8 == 0:
                start = pl.multiple_of(start, 8)
            ref = outs[at_out]
            ref[...] = flat[pl.ds(start, rows), :].astype(ref.dtype)
            at_out += 1


def message_kernel(w_ref, *refs):
    both, mats, hots = refs[0:2], refs[2:4], refs[4:6]
    out_ref, flat, in_ref, res_ref, wide_ref = refs[6:]
    n = out_ref.shape[0]
    slots = in_ref.shape[1]
    part = w_ref.shape[0] // 16
    for p in range(16):
        flat[p * part : (p + 1) * part, :] = w_ref[p * part : (p + 1) * part, :].astype(F32)

    def h(first, end):
        return jnp.concatenate(
            [r[: r.shape[0] // 2, first * 128 : end * 128] for r in both], axis=0
        )

    def fill(j, wide):
        for i in range(wide.shape[1] // 128):
            in_ref[j + i] = wide[:, 128 * i : 128 * i + 128]

    def weight(base, width, b, many):
        parts = [
            flat[pl.ds(base + b + t, width * 128, stride=width), :].astype(BF16)
            for t in range(many)
        ]
        return parts[0] if many == 1 else jnp.concatenate(parts, axis=1)

    def rounded(v):
        return v.astype(BF16).astype(F32)

    def pairs(width):
        return [(b, min(2, width - b)) for b in range(0, width, 2)]

    h0 = h(0, 7)
    for b, many in pairs(7):
        fill(b, rounded(dot(h0, weight(0, 7, b, many))))
    base = 49 * 128
    for first, width in ((7, 6), (19, 5)):
        mid, end = first + width, first + 2 * width
        pair = jnp.concatenate([h(first, mid), h(mid, end)], axis=0)
        for b, many in pairs(width):
            real = dot(pair, weight(base, width, b, many))
            imag = dot(pair, weight(base + width * width * 128, width, b, many))
            fill(first + b, rounded(real[:slots] - imag[slots:]))
            fill(mid + b, rounded(imag[:slots] + real[slots:]))
        base += 2 * width * width * 128
    for j in range(K, 32):
        in_ref[j] = jnp.zeros((slots, 128), F32)
    at = 0
    for m in mats:
        size = m.shape[0] * 8
        turn(m, in_ref.at[:, at : at + size, :], res_ref.at[:, at : at + size, :])
        at += size
    for k in range(K):
        wide_ref[:, k * 128 : (k + 1) * 128] = res_ref[k].astype(BF16)
    target = jnp.concatenate([r[...] for r in hots], axis=0).astype(F32).T.astype(BF16)
    for j, w in chunks():
        cols = slice(j * 128, (j + w) * 128)
        out_ref[:, cols] = dot(target, wide_ref[:, cols]).astype(BF16)


def shape(dims, kind):
    return jax.ShapeDtypeStruct(dims, kind)


def whole(like):
    zeros = (0,) * len(like.shape)
    return pl.BlockSpec(like.shape, lambda i: zeros, pipeline_mode=pl.Buffered(1))


def call(kernel, name, mib, outs, operands, scratch=(), numbers=None, cost=None):
    first = [] if numbers is None else [pl.BlockSpec(memory_space=pltpu.SMEM)]
    return pl.pallas_call(
        kernel,
        grid=(1,),
        out_shape=outs,
        in_specs=first + [whole(v) for v in operands],
        out_specs=[whole(o) for o in outs],
        scratch_shapes=list(scratch),
        compiler_params=pltpu.CompilerParams(vmem_limit_bytes=mib * 1024 * 1024),
        cost_estimate=cost,
        name=name,
    )(*(() if numbers is None else (numbers,)), *operands)


def on_device(
    n_z, n_x, node_feats, node_grad, flat_params, rot_table, edge_src, edge_dst, edge_rot,
    edge_owner,
):
    n = edge_src.shape[0]
    cap = n // 4
    width = node_feats.shape[1]
    rows = flat_params.shape[0]
    n_dp = n_z * n_x * 2
    n_rot = rot_table.shape[0]
    me = dp_index(n_x)
    smem = pl.BlockSpec(memory_space=pltpu.SMEM)

    def shift(block, step):
        route = [
            (i, i + step) for i in range(n_dp)
            if 0 <= i + step and i // SPAN == (i + step) // SPAN
        ]
        return lax.ppermute(block, ALL, route)

    def swap(block):
        return lax.ppermute(block, "core", [(0, 1), (1, 0)])

    weights = lax.all_gather(flat_params, ALL, axis=0, tiled=True)

    row = lambda v: v.reshape(1, n)
    here, *outbound = call(
        send_kernel, "send", 62,
        [shape((n // 2, width + 128), BF16)] + [shape((cap, width + 128), BF16)] * 4,
        [row(edge_owner), row(edge_src), row(edge_dst), row(edge_rot), node_feats],
        numbers=me.reshape(1),
    )
    arrived = [shift(r, s) for r, s in zip(outbound, STEPS)]

    tab = rot_table.transpose(1, 0, 2).reshape(K * n_rot, K)
    tabt = rot_table.transpose(2, 0, 1).reshape(K * n_rot, K)

    def rotate(rows_in, name, cost=None):
        slots = sum(r.shape[0] for r in rows_in)
        return call(
            lambda *refs: rotate_kernel(len(rows_in), *refs), name, 62,
            [
                shape((2 * slots, width), BF16), shape((slots, n), BF16),
                shape((slots, n_rot), BF16),
            ],
            [*rows_in, tab, node_grad],
            [
                pltpu.VMEM((slots // 8, 240, 256), BF16), pltpu.VMEM((30, slots, 256), F32),
                pltpu.VMEM((32, slots, 256), F32), pltpu.VMEM((30, slots, 256), F32),
            ],
            cost=cost,
        )

    both_a, hot_a, turn_a = rotate([here] + arrived[:2], "rotate_first")
    both_a_other = swap(both_a)
    last, both_a = lax.optimization_barrier((arrived[2:], both_a))
    both_b, hot_b, turn_b = rotate(
        last, "rotate_last",
        pl.CostEstimate(flops=10**10, bytes_accessed=10**8, transcendentals=0),
    )
    both_b_other = swap(both_b)
    both, hots, turns = [both_a, both_b], [hot_a, hot_b], [turn_a, turn_b]

    n_send = n_z * (n_x - 1)
    blocks = call(
        lambda *refs: grad_kernel(n_z, n_x, *refs), "weight_terms", 62,
        [shape((rows, 128), BF16)] * n_send + [shape((rows, 128), F32)] * n_z,
        both + [both_a_other, both_b_other],
        [pltpu.VMEM((rows * n_dp, 128), F32)],
        numbers=me.reshape(1),
    )
    turns, blocks = lax.optimization_barrier((turns, list(blocks)))
    mats = call(
        back_kernel, "back", 62,
        [shape((t.shape[0] // 8, 240, 256), BF16) for t in turns],
        [tabt] + turns,
        [pltpu.VMEM((30, t.shape[0], 256), F32) for t in turns],
    )
    kept = blocks[n_send:]
    kept[0], mats = lax.optimization_barrier((kept[0], mats))
    sums = {}
    for at, r in enumerate(reversed(range(n_z))):
        total = kept[at]
        for o in range(1, n_x):
            got = lax.ppermute(
                blocks[(o - 1) * n_z + at], "x", [(s, (s + o) % n_x) for s in range(n_x)]
            )
            total = total + got.astype(F32)
        sums[r] = total
    for bit in [1 << i for i in range(n_z.bit_length() - 1)]:
        for r in reversed(range(bit, n_z, 2 * bit)):
            term = sums[r].astype(BF16)
            if (bit, r) == (1, 1):
                last_term = term
            got = lax.ppermute(term, "z", [(s, s ^ bit) for s in range(n_z)])
            if 2 * bit < n_z:
                sums[r ^ bit] = sums[r ^ bit] + got.astype(F32)
    weights, _ = lax.optimization_barrier((weights, last_term))
    slots = n // 2 + 4 * cap
    (node_out,) = call(
        message_kernel, "messages", 62,
        [shape((n, width), BF16)],
        [weights, *both, *mats, *hots],
        [
            pltpu.VMEM((rows * n_dp, 128), F32), pltpu.VMEM((32, slots, 128), F32),
            pltpu.VMEM((30, slots, 128), F32), pltpu.VMEM((slots, width), BF16),
        ],
    )
    got, node_out = lax.optimization_barrier((got, node_out))
    result = sums[0] + got.astype(F32)
    weight_grad = result * (1.0 / math.sqrt(n * n_dp))
    return (node_out, weight_grad)


def chips(mesh):
    n_dp = mesh.shape["dp"]
    line = list(mesh.devices.reshape(-1, n_dp)[0])
    coords = [getattr(d, "coords", None) for d in line]
    n_x = 2 if coords[0] is None else len({c[0] for c in coords})
    return n_dp // (2 * n_x), n_x


def solution(mesh):
    n_z, n_x = chips(mesh)
    fine = Mesh(
        np.asarray(mesh.devices).reshape(mesh.shape["groups"], n_z, n_x, 2),
        ("groups", "z", "x", "core"),
    )
    every = ("groups",) + ALL
    placed = (
        P(every, None),
        P(every, None),
        P(ALL, None),
        P(),
        P(every),
        P(every),
        P(every),
        P(every, None),
    )
    return jax.shard_map(
        lambda *args: on_device(n_z, n_x, *args),
        mesh=fine,
        in_specs=placed,
        out_specs=(P(every, None), P(every, None)),
        check_vma=False,
    )
```

```python
import math

import jax
import jax.numpy as jnp
import numpy as np
from jax import lax
from jax.experimental import pallas as pl
from jax.experimental.pallas import tpu as pltpu
from jax.sharding import Mesh, PartitionSpec as P

K = 29
SPAN = 8
STEPS = (-2, 2, -1, 1)
F32 = jnp.float32
BF16 = jnp.bfloat16
ALL = ("z", "x", "core")


def dot(a, b):
    return jnp.dot(a, b, preferred_element_type=F32)


def iota(shape, dim):
    return lax.broadcasted_iota(jnp.int32, shape, dim)


def hot(cond):
    return jnp.where(cond, 1.0, 0.0).astype(BF16)


def column(row):
    n = row.shape[1]
    eye = iota((n, n), 0) == iota((n, n), 1)
    return jnp.sum(jnp.where(eye, row.astype(F32), 0.0), axis=1, keepdims=True)


def dp_index(n_x):
    return (lax.axis_index("z") * n_x + lax.axis_index("x")) * 2 + lax.axis_index("core")


def send_kernel(me_ref, owner_ref, src_ref, dst_ref, rot_ref, feats_ref, *outs):
    n = feats_ref.shape[0]
    width = feats_ref.shape[1]
    half, cap = n // 2, n // 4
    off_row = (owner_ref[...] - me_ref[0]).astype(F32)
    off = column(off_row)
    before = (off == off_row) & (iota((n, n), 0) < iota((n, n), 1))
    slot = jnp.sum(jnp.where(before, 1.0, 0.0), axis=0, keepdims=True)
    for q, step in enumerate(STEPS):
        slot = jnp.where(off_row == step, slot + float(half + q * cap), slot)
    slots = half + 4 * cap
    here = slot == iota((slots, n), 0).astype(F32)

    def pick(row):
        return jnp.sum(jnp.where(here, row, 0.0), axis=1, keepdims=True)

    source = pick(src_ref[...].astype(F32) + 1.0) - 1.0
    target = pick(dst_ref[...].astype(F32) + 1.0)
    turns = pick(rot_ref[...].astype(F32))
    source_hot = hot(source == iota((slots, n), 1).astype(F32))
    lane = iota((slots, 128), 1)
    ids = jnp.where(lane == 0, target, jnp.where(lane == 1, turns, 0.0)).astype(BF16)
    spans = [(0, half)] + [(half + q * cap, cap) for q in range(4)]
    for o, (at, size) in zip(outs, spans):
        o[:, width:] = ids[at : at + size]
    for j, w in chunks():
        cols = slice(j * 128, (j + w) * 128)
        rows = dot(source_hot, feats_ref[:, cols]).astype(BF16)
        for o, (at, size) in zip(outs, spans):
            o[:, cols] = rows[at : at + size]


def turn(mats_ref, src_ref, res_ref):
    lanes = src_ref.shape[2]
    for g in range(src_ref.shape[1] // 8):
        rhs = src_ref[:, 8 * g : 8 * g + 8, :].reshape(256, lanes).astype(BF16)
        res = dot(mats_ref[g], rhs)
        res_ref[:, 8 * g : 8 * g + 8, :] = res.reshape(30, 8, lanes)


def build(table_ref, rot_hot, mats_ref, tmp_ref):
    n = rot_hot.shape[0]
    n_rot = rot_hot.shape[1]
    spread = hot(iota((K, 256), 1) // 8 == iota((K, 256), 0))
    wide = dot(table_ref[...], spread).astype(BF16)
    own = (iota((n, 256), 1) % 8) == (iota((n, 256), 0) % 8)
    for k in range(K):
        tmp_ref[k] = jnp.where(own, dot(rot_hot, wide[k * n_rot : (k + 1) * n_rot]), 0.0)
    tmp_ref[K] = jnp.zeros((n, 256), F32)
    for g in range(n // 8):
        mats_ref[g] = tmp_ref[:, 8 * g : 8 * g + 8, :].reshape(240, 256).astype(BF16)


def chunks():
    j = 0
    while j < K:
        w = min(4, K - j)
        yield j, w
        j += w


def joined(refs, cols):
    return jnp.concatenate([r[:, cols] for r in refs], axis=0)


def number(ids, lane):
    at = iota(ids.shape, 1) == lane
    return jnp.sum(jnp.where(at, ids.astype(F32), 0.0), axis=1, keepdims=True)


def rotate_kernel(count, *refs):
    raw, (tab_ref, grad_ref) = refs[:count], refs[count : count + 2]
    both_ref, hot_ref, turn_ref, mats_ref, tmp_ref, in_ref, res_ref = refs[count + 2 :]
    n = grad_ref.shape[0]
    n_rot = tab_ref.shape[0] // K
    width = grad_ref.shape[1]
    ids = joined(raw, slice(width, width + 128))
    slots = ids.shape[0]
    target_hot = hot(number(ids, 0) - 1.0 == iota((slots, n), 1).astype(F32))
    rot_hot = hot(number(ids, 1) == iota((slots, n_rot), 1).astype(F32))
    hot_ref[...] = target_hot
    turn_ref[...] = rot_hot
    for j, w in chunks():
        cols = slice(j * 128, (j + w) * 128)
        rows = joined(raw, cols).astype(F32)
        back = dot(target_hot, grad_ref[:, cols])
        for i in range(w):
            in_ref[j + i, :, :128] = rows[:, 128 * i : 128 * i + 128]
            in_ref[j + i, :, 128:] = back[:, 128 * i : 128 * i + 128]
    for j in range(K, 32):
        in_ref[j] = jnp.zeros((slots, 256), F32)
    build(tab_ref, rot_hot, mats_ref, tmp_ref)
    turn(mats_ref, in_ref, res_ref)
    for k in range(K):
        cols = slice(k * 128, (k + 1) * 128)
        both_ref[:slots, cols] = res_ref[k, :, :128].astype(BF16)
        both_ref[slots:, cols] = res_ref[k, :, 128:].astype(BF16)


def back_kernel(tabt_ref, *refs):
    for i in range(2):
        build(tabt_ref, refs[i][...], refs[2 + i], refs[4 + i])


def grad_kernel(n_z, n_x, me_ref, *refs):
    parts, outs, flat = refs[:4], refs[4:-1], refs[-1]
    chip, core = me_ref[0] // 2, me_ref[0] % 2
    z, x = chip // n_x, chip % n_x

    def left(first, width):
        at = slice(first * 128, (first + width) * 128)
        return [p[: p.shape[0] // 2, at] for p in parts]

    def right(first, width):
        at = slice(first * 128, (first + width) * 128)
        return [p[p.shape[0] // 2 :, at] for p in parts]

    def outer(lhs, rhs):
        return lax.dot_general(lhs, rhs, (((0,), (0,)), ((), ())), preferred_element_type=F32)

    def emit(base, width, res):
        for b in range(width):
            flat[pl.ds(base + b, width * 128, stride=width), :] = res[:, b * 128 : (b + 1) * 128]

    emit(0, 7, outer(jnp.concatenate(left(0, 7), axis=0), jnp.concatenate(right(0, 7), axis=0)))
    base = 49 * 128
    for first, width in ((7, 6), (19, 5)):
        lhs = jnp.concatenate(left(first, width) + left(first + width, width), axis=0)
        real, imag = right(first, width), right(first + width, width)
        emit(base, width, outer(lhs, jnp.concatenate(real + imag, axis=0)))
        base += width * width * 128
        emit(base, width, outer(lhs, jnp.concatenate(imag + [-v for v in real], axis=0)))
        base += width * width * 128

    rows = outs[0].shape[0]
    for o in list(range(1, n_x)) + [0]:
        for r in reversed(range(n_z)):
            start = (((z ^ r) * n_x + (x + o) % n_x) * 2 + core) * rows
            if rows % 8 == 0:
                start = pl.multiple_of(start, 8)
            block = flat[pl.ds(start, rows), :]
            if o == 0:
                outs[-1 - r][...] = block
            elif r < 2:
                outs[(o - 1) * (n_z - 1) + n_z - 2][1 - r] = block.astype(BF16)
            else:
                outs[(o - 1) * (n_z - 1) + n_z - 1 - r][...] = block.astype(BF16)


def message_kernel(rows, place_ref, *refs):
    pieces, both, mats, hots = refs[0:3], refs[3:5], refs[5:7], refs[7:9]
    out_ref, flat, in_ref, res_ref, wide_ref = refs[9:]
    n = out_ref.shape[0]
    slots = in_ref.shape[1]
    group, core = place_ref[0], place_ref[1]
    half = pieces[1].shape[0]
    for ref, which, first in zip(
        pieces, (group, 1 - group, 1 - group), (0, core * half, (1 - core) * half)
    ):
        size = ref.shape[1]
        for i in range(ref.shape[0]):
            start = (first + i) * rows + which * (rows - size)
            if rows % 8 == 0:
                start = pl.multiple_of(start, 8)
            flat[pl.ds(start, size), :] = ref[i].astype(F32)

    def h(first, end):
        return jnp.concatenate(
            [r[: r.shape[0] // 2, first * 128 : end * 128] for r in both], axis=0
        )

    def fill(j, wide):
        for i in range(wide.shape[1] // 128):
            in_ref[j + i] = wide[:, 128 * i : 128 * i + 128]

    def weight(base, width, b, many):
        parts = [
            flat[pl.ds(base + b + t, width * 128, stride=width), :].astype(BF16)
            for t in range(many)
        ]
        return parts[0] if many == 1 else jnp.concatenate(parts, axis=1)

    def rounded(v):
        return v.astype(BF16).astype(F32)

    def pairs(width):
        return [(b, min(2, width - b)) for b in range(0, width, 2)]

    h0 = h(0, 7)
    for b, many in pairs(7):
        fill(b, rounded(dot(h0, weight(0, 7, b, many))))
    base = 49 * 128
    for first, width in ((7, 6), (19, 5)):
        mid, end = first + width, first + 2 * width
        pair = jnp.concatenate([h(first, mid), h(mid, end)], axis=0)
        for b, many in pairs(width):
            real = dot(pair, weight(base, width, b, many))
            imag = dot(pair, weight(base + width * width * 128, width, b, many))
            fill(first + b, rounded(real[:slots] - imag[slots:]))
            fill(mid + b, rounded(imag[:slots] + real[slots:]))
        base += 2 * width * width * 128
    for j in range(K, 32):
        in_ref[j] = jnp.zeros((slots, 128), F32)
    at = 0
    for m in mats:
        size = m.shape[0] * 8
        turn(m, in_ref.at[:, at : at + size, :], res_ref.at[:, at : at + size, :])
        at += size
    for k in range(K):
        wide_ref[:, k * 128 : (k + 1) * 128] = res_ref[k].astype(BF16)
    target = jnp.concatenate([r[...] for r in hots], axis=0).astype(F32).T.astype(BF16)
    for j, w in chunks():
        cols = slice(j * 128, (j + w) * 128)
        out_ref[:, cols] = dot(target, wide_ref[:, cols]).astype(BF16)


def shape(dims, kind):
    return jax.ShapeDtypeStruct(dims, kind)


def whole(like):
    zeros = (0,) * len(like.shape)
    return pl.BlockSpec(like.shape, lambda i: zeros, pipeline_mode=pl.Buffered(1))


def call(kernel, name, mib, outs, operands, scratch=(), numbers=None, cost=None):
    first = [] if numbers is None else [pl.BlockSpec(memory_space=pltpu.SMEM)]
    return pl.pallas_call(
        kernel,
        grid=(1,),
        out_shape=outs,
        in_specs=first + [whole(v) for v in operands],
        out_specs=[whole(o) for o in outs],
        scratch_shapes=list(scratch),
        compiler_params=pltpu.CompilerParams(vmem_limit_bytes=mib * 1024 * 1024),
        cost_estimate=cost,
        name=name,
    )(*(() if numbers is None else (numbers,)), *operands)


def on_device(
    n_z, n_x, node_feats, node_grad, flat_params, rot_table, edge_src, edge_dst, edge_rot,
    edge_owner,
):
    n = edge_src.shape[0]
    cap = n // 4
    width = node_feats.shape[1]
    rows = flat_params.shape[0]
    n_dp = n_z * n_x * 2
    n_rot = rot_table.shape[0]
    me = dp_index(n_x)
    smem = pl.BlockSpec(memory_space=pltpu.SMEM)

    def shift(block, step):
        route = [
            (i, i + step) for i in range(n_dp)
            if 0 <= i + step and i // SPAN == (i + step) // SPAN
        ]
        return lax.ppermute(block, ALL, route)

    def swap(block):
        return lax.ppermute(block, "core", [(0, 1), (1, 0)])

    group, core = lax.axis_index("groups"), lax.axis_index("core")
    piece = -(-rows // 32) * 16
    part = lax.dynamic_slice_in_dim(flat_params, group * (rows - piece), piece, 0)
    gathered = lax.all_gather(part, ALL, axis=0)
    mine = lax.dynamic_slice_in_dim(gathered, core * (n_dp // 2), n_dp // 2, 0)

    row = lambda v: v.reshape(1, n)
    here, *outbound = call(
        send_kernel, "send", 62,
        [shape((n // 2, width + 128), BF16)] + [shape((cap, width + 128), BF16)] * 4,
        [row(edge_owner), row(edge_src), row(edge_dst), row(edge_rot), node_feats],
        numbers=me.reshape(1),
    )
    arrived = [shift(r, s) for r, s in zip(outbound, STEPS)]

    tab = rot_table.transpose(1, 0, 2).reshape(K * n_rot, K)
    tabt = rot_table.transpose(2, 0, 1).reshape(K * n_rot, K)

    def rotate(rows_in, name, cost=None):
        slots = sum(r.shape[0] for r in rows_in)
        return call(
            lambda *refs: rotate_kernel(len(rows_in), *refs), name, 62,
            [
                shape((2 * slots, width), BF16), shape((slots, n), BF16),
                shape((slots, n_rot), BF16),
            ],
            [*rows_in, tab, node_grad],
            [
                pltpu.VMEM((slots // 8, 240, 256), BF16), pltpu.VMEM((30, slots, 256), F32),
                pltpu.VMEM((32, slots, 256), F32), pltpu.VMEM((30, slots, 256), F32),
            ],
            cost=cost,
        )

    both_a, hot_a, turn_a = rotate([here] + arrived[:2], "rotate_first")
    both_a_other = swap(both_a)
    last, both_a = lax.optimization_barrier((arrived[2:], both_a))
    both_b, hot_b, turn_b = rotate(
        last, "rotate_last",
        pl.CostEstimate(flops=10**10, bytes_accessed=10**8, transcendentals=0),
    )
    both_b_other = swap(both_b)
    both_b_other, mine = lax.optimization_barrier((both_b_other, mine))
    crossed = lax.ppermute(mine, "groups", [(0, 1), (1, 0)])
    both, hots, turns = [both_a, both_b], [hot_a, hot_b], [turn_a, turn_b]

    n_send = (n_z - 1) * (n_x - 1)
    sends = [shape((rows, 128), BF16)] * (n_z - 2) + [shape((2, rows, 128), BF16)]
    blocks = call(
        lambda *refs: grad_kernel(n_z, n_x, *refs), "weight_terms", 62,
        sends * (n_x - 1) + [shape((rows, 128), F32)] * n_z,
        both + [both_a_other, both_b_other],
        [pltpu.VMEM((rows * n_dp, 128), F32)],
        numbers=me.reshape(1),
    )
    turns, blocks = lax.optimization_barrier((turns, list(blocks)))
    mats = call(
        back_kernel, "back", 62,
        [shape((t.shape[0] // 8, 240, 256), BF16) for t in turns],
        [tabt] + turns,
        [pltpu.VMEM((30, t.shape[0], 256), F32) for t in turns],
    )
    kept = blocks[n_send:]
    kept[0], mats = lax.optimization_barrier((kept[0], mats))
    sums = {r: kept[n_z - 1 - r] for r in range(n_z)}
    for at in range(n_z - 1):
        for o in range(1, n_x):
            got = lax.ppermute(
                blocks[(o - 1) * (n_z - 1) + at], "x", [(s, (s + o) % n_x) for s in range(n_x)]
            ).astype(F32)
            if at < n_z - 2:
                sums[n_z - 1 - at] += got
            else:
                sums[1] += got[0]
                sums[0] += got[1]
    terms = []
    for bit in [1 << i for i in range(n_z.bit_length() - 1)]:
        for r in reversed(range(bit, n_z, 2 * bit)):
            term = sums[r].astype(BF16)
            if bit == 1:
                terms.append(term)
            got = lax.ppermute(term, "z", [(s, s ^ bit) for s in range(n_z)])
            if 2 * bit < n_z:
                sums[r ^ bit] = sums[r ^ bit] + got.astype(F32)
    crossed, _ = lax.optimization_barrier((crossed, terms[0]))
    swapped, _ = lax.optimization_barrier((swap(crossed), terms[-1]))
    slots = n // 2 + 4 * cap
    (node_out,) = call(
        lambda *refs: message_kernel(rows, *refs), "messages", 62,
        [shape((n, width), BF16)],
        [gathered, crossed, swapped, *both, *mats, *hots],
        [
            pltpu.VMEM((rows * n_dp, 128), F32), pltpu.VMEM((32, slots, 128), F32),
            pltpu.VMEM((30, slots, 128), F32), pltpu.VMEM((slots, width), BF16),
        ],
        numbers=jnp.stack([group, core]),
    )
    got, node_out = lax.optimization_barrier((got, node_out))
    result = sums[0] + got.astype(F32)
    weight_grad = result * (1.0 / math.sqrt(n * n_dp))
    return (node_out, weight_grad)


def chips(mesh):
    n_dp = mesh.shape["dp"]
    line = list(mesh.devices.reshape(-1, n_dp)[0])
    coords = [getattr(d, "coords", None) for d in line]
    n_x = 2 if coords[0] is None else len({c[0] for c in coords})
    return n_dp // (2 * n_x), n_x


def solution(mesh):
    n_z, n_x = chips(mesh)
    fine = Mesh(
        np.asarray(mesh.devices).reshape(mesh.shape["groups"], n_z, n_x, 2),
        ("groups", "z", "x", "core"),
    )
    every = ("groups",) + ALL
    placed = (
        P(every, None),
        P(every, None),
        P(ALL, None),
        P(),
        P(every),
        P(every),
        P(every),
        P(every, None),
    )
    return jax.shard_map(
        lambda *args: on_device(n_z, n_x, *args),
        mesh=fine,
        in_specs=placed,
        out_specs=(P(every, None), P(every, None)),
        check_vma=False,
    )
```

```python
import math

import jax
import jax.numpy as jnp
import numpy as np
from jax import lax
from jax.experimental import pallas as pl
from jax.experimental.pallas import tpu as pltpu
from jax.sharding import Mesh, PartitionSpec as P

K = 29
SPAN = 8
STEPS = (-2, 2, -1, 1)
F32 = jnp.float32
BF16 = jnp.bfloat16
ALL = ("z", "x", "core")


def dot(a, b):
    return jnp.dot(a, b, preferred_element_type=F32)


def iota(shape, dim):
    return lax.broadcasted_iota(jnp.int32, shape, dim)


def hot(cond):
    return jnp.where(cond, 1.0, 0.0).astype(BF16)


def column(row):
    n = row.shape[1]
    eye = iota((n, n), 0) == iota((n, n), 1)
    return jnp.sum(jnp.where(eye, row.astype(F32), 0.0), axis=1, keepdims=True)


def dp_index(n_x):
    return (lax.axis_index("z") * n_x + lax.axis_index("x")) * 2 + lax.axis_index("core")


def send_kernel(me_ref, owner_ref, src_ref, dst_ref, rot_ref, feats_ref, *outs):
    n = feats_ref.shape[0]
    width = feats_ref.shape[1]
    half, cap = n // 2, n // 4
    off_row = (owner_ref[...] - me_ref[0]).astype(F32)
    off = column(off_row)
    before = (off == off_row) & (iota((n, n), 0) < iota((n, n), 1))
    slot = jnp.sum(jnp.where(before, 1.0, 0.0), axis=0, keepdims=True)
    for q, step in enumerate(STEPS):
        slot = jnp.where(off_row == step, slot + float(half + q * cap), slot)
    slots = half + 4 * cap
    here = slot == iota((slots, n), 0).astype(F32)

    def pick(row):
        return jnp.sum(jnp.where(here, row, 0.0), axis=1, keepdims=True)

    source = pick(src_ref[...].astype(F32) + 1.0) - 1.0
    target = pick(dst_ref[...].astype(F32) + 1.0)
    turns = pick(rot_ref[...].astype(F32))
    source_hot = hot(source == iota((slots, n), 1).astype(F32))
    lane = iota((slots, 128), 1)
    ids = jnp.where(lane == 0, target, jnp.where(lane == 1, turns, 0.0)).astype(BF16)
    spans = [(0, half)] + [(half + q * cap, cap) for q in range(4)]
    for o, (at, size) in zip(outs, spans):
        o[:, width:] = ids[at : at + size]
    for j, w in chunks():
        cols = slice(j * 128, (j + w) * 128)
        rows = dot(source_hot, feats_ref[:, cols]).astype(BF16)
        for o, (at, size) in zip(outs, spans):
            o[:, cols] = rows[at : at + size]


def turn(mats_ref, src_ref, res_ref):
    lanes = src_ref.shape[2]
    for g in range(src_ref.shape[1] // 8):
        rhs = src_ref[:, 8 * g : 8 * g + 8, :].reshape(256, lanes).astype(BF16)
        res = dot(mats_ref[g], rhs)
        res_ref[:, 8 * g : 8 * g + 8, :] = res.reshape(30, 8, lanes)


def build(table_ref, rot_hot, mats_ref, tmp_ref):
    n = rot_hot.shape[0]
    n_rot = rot_hot.shape[1]
    spread = hot(iota((K, 256), 1) // 8 == iota((K, 256), 0))
    wide = dot(table_ref[...], spread).astype(BF16)
    own = (iota((n, 256), 1) % 8) == (iota((n, 256), 0) % 8)
    for k in range(K):
        tmp_ref[k] = jnp.where(own, dot(rot_hot, wide[k * n_rot : (k + 1) * n_rot]), 0.0)
    tmp_ref[K] = jnp.zeros((n, 256), F32)
    for g in range(n // 8):
        mats_ref[g] = tmp_ref[:, 8 * g : 8 * g + 8, :].reshape(240, 256).astype(BF16)


def chunks():
    j = 0
    while j < K:
        w = min(4, K - j)
        yield j, w
        j += w


def joined(refs, cols):
    return jnp.concatenate([r[:, cols] for r in refs], axis=0)


def number(ids, lane):
    at = iota(ids.shape, 1) == lane
    return jnp.sum(jnp.where(at, ids.astype(F32), 0.0), axis=1, keepdims=True)


def rotate_kernel(count, *refs):
    raw, (tab_ref, grad_ref) = refs[:count], refs[count : count + 2]
    both_ref, hot_ref, turn_ref, mats_ref, tmp_ref, in_ref, res_ref = refs[count + 2 :]
    n = grad_ref.shape[0]
    n_rot = tab_ref.shape[0] // K
    width = grad_ref.shape[1]
    ids = joined(raw, slice(width, width + 128))
    slots = ids.shape[0]
    target_hot = hot(number(ids, 0) - 1.0 == iota((slots, n), 1).astype(F32))
    rot_hot = hot(number(ids, 1) == iota((slots, n_rot), 1).astype(F32))
    hot_ref[...] = target_hot
    turn_ref[...] = rot_hot
    for j, w in chunks():
        cols = slice(j * 128, (j + w) * 128)
        rows = joined(raw, cols).astype(F32)
        back = dot(target_hot, grad_ref[:, cols])
        for i in range(w):
            in_ref[j + i, :, :128] = rows[:, 128 * i : 128 * i + 128]
            in_ref[j + i, :, 128:] = back[:, 128 * i : 128 * i + 128]
    for j in range(K, 32):
        in_ref[j] = jnp.zeros((slots, 256), F32)
    build(tab_ref, rot_hot, mats_ref, tmp_ref)
    turn(mats_ref, in_ref, res_ref)
    for k in range(K):
        cols = slice(k * 128, (k + 1) * 128)
        both_ref[:slots, cols] = res_ref[k, :, :128].astype(BF16)
        both_ref[slots:, cols] = res_ref[k, :, 128:].astype(BF16)


def back_kernel(tabt_ref, *refs):
    for i in range(2):
        build(tabt_ref, refs[i][...], refs[2 + i], refs[4 + i])


def square(n_x):
    return [(b, o) for b in (1, 0) for o in reversed(range(n_x)) if (b, o) != (0, 0)]


def placed_blocks(n_z, n_x):
    pairs = list(reversed(range(0, n_z, 2)))
    return [(r + b, o) for r in pairs for b, o in square(n_x)] + [(r, 0) for r in pairs]


def grad_kernel(n_z, n_x, me_ref, *refs):
    parts, outs, flat = refs[:4], refs[4:-1], refs[-1]
    chip, core = me_ref[0] // 2, me_ref[0] % 2
    z, x = chip // n_x, chip % n_x

    def left(first, width):
        at = slice(first * 128, (first + width) * 128)
        return [p[: p.shape[0] // 2, at] for p in parts]

    def right(first, width):
        at = slice(first * 128, (first + width) * 128)
        return [p[p.shape[0] // 2 :, at] for p in parts]

    def outer(lhs, rhs):
        return lax.dot_general(lhs, rhs, (((0,), (0,)), ((), ())), preferred_element_type=F32)

    def emit(base, width, res):
        for b in range(width):
            flat[pl.ds(base + b, width * 128, stride=width), :] = res[:, b * 128 : (b + 1) * 128]

    emit(0, 7, outer(jnp.concatenate(left(0, 7), axis=0), jnp.concatenate(right(0, 7), axis=0)))
    base = 49 * 128
    for first, width in ((7, 6), (19, 5)):
        lhs = jnp.concatenate(left(first, width) + left(first + width, width), axis=0)
        real, imag = right(first, width), right(first + width, width)
        emit(base, width, outer(lhs, jnp.concatenate(real + imag, axis=0)))
        base += width * width * 128
        emit(base, width, outer(lhs, jnp.concatenate(imag + [-v for v in real], axis=0)))
        base += width * width * 128

    rows = outs[0].shape[0]
    for ref, (r, o) in zip(outs, placed_blocks(n_z, n_x)):
        start = (((z ^ r) * n_x + (x + o) % n_x) * 2 + core) * rows
        if rows % 8 == 0:
            start = pl.multiple_of(start, 8)
        ref[...] = flat[pl.ds(start, rows), :].astype(ref.dtype)


def message_kernel(w_ref, *refs):
    both, mats, hots = refs[0:2], refs[2:4], refs[4:6]
    out_ref, flat, in_ref, res_ref, wide_ref = refs[6:]
    n = out_ref.shape[0]
    slots = in_ref.shape[1]
    part = w_ref.shape[0] // 16
    for p in range(16):
        flat[p * part : (p + 1) * part, :] = w_ref[p * part : (p + 1) * part, :].astype(F32)

    def h(first, end):
        return jnp.concatenate(
            [r[: r.shape[0] // 2, first * 128 : end * 128] for r in both], axis=0
        )

    def fill(j, wide):
        for i in range(wide.shape[1] // 128):
            in_ref[j + i] = wide[:, 128 * i : 128 * i + 128]

    def weight(base, width, b, many):
        parts = [
            flat[pl.ds(base + b + t, width * 128, stride=width), :].astype(BF16)
            for t in range(many)
        ]
        return parts[0] if many == 1 else jnp.concatenate(parts, axis=1)

    def rounded(v):
        return v.astype(BF16).astype(F32)

    def pairs(width):
        return [(b, min(2, width - b)) for b in range(0, width, 2)]

    h0 = h(0, 7)
    for b, many in pairs(7):
        fill(b, rounded(dot(h0, weight(0, 7, b, many))))
    base = 49 * 128
    for first, width in ((7, 6), (19, 5)):
        mid, end = first + width, first + 2 * width
        pair = jnp.concatenate([h(first, mid), h(mid, end)], axis=0)
        for b, many in pairs(width):
            real = dot(pair, weight(base, width, b, many))
            imag = dot(pair, weight(base + width * width * 128, width, b, many))
            fill(first + b, rounded(real[:slots] - imag[slots:]))
            fill(mid + b, rounded(imag[:slots] + real[slots:]))
        base += 2 * width * width * 128
    for j in range(K, 32):
        in_ref[j] = jnp.zeros((slots, 128), F32)
    at = 0
    for m in mats:
        size = m.shape[0] * 8
        turn(m, in_ref.at[:, at : at + size, :], res_ref.at[:, at : at + size, :])
        at += size
    for k in range(K):
        wide_ref[:, k * 128 : (k + 1) * 128] = res_ref[k].astype(BF16)
    target = jnp.concatenate([r[...] for r in hots], axis=0).astype(F32).T.astype(BF16)
    for j, w in chunks():
        cols = slice(j * 128, (j + w) * 128)
        out_ref[:, cols] = dot(target, wide_ref[:, cols]).astype(BF16)


def shape(dims, kind):
    return jax.ShapeDtypeStruct(dims, kind)


def whole(like):
    zeros = (0,) * len(like.shape)
    return pl.BlockSpec(like.shape, lambda i: zeros, pipeline_mode=pl.Buffered(1))


def call(kernel, name, mib, outs, operands, scratch=(), numbers=None, cost=None):
    first = [] if numbers is None else [pl.BlockSpec(memory_space=pltpu.SMEM)]
    return pl.pallas_call(
        kernel,
        grid=(1,),
        out_shape=outs,
        in_specs=first + [whole(v) for v in operands],
        out_specs=[whole(o) for o in outs],
        scratch_shapes=list(scratch),
        compiler_params=pltpu.CompilerParams(vmem_limit_bytes=mib * 1024 * 1024),
        cost_estimate=cost,
        name=name,
    )(*(() if numbers is None else (numbers,)), *operands)


def on_device(
    n_z, n_x, node_feats, node_grad, flat_params, rot_table, edge_src, edge_dst, edge_rot,
    edge_owner,
):
    n = edge_src.shape[0]
    cap = n // 4
    width = node_feats.shape[1]
    rows = flat_params.shape[0]
    n_dp = n_z * n_x * 2
    n_rot = rot_table.shape[0]
    me = dp_index(n_x)
    smem = pl.BlockSpec(memory_space=pltpu.SMEM)

    def shift(block, step):
        route = [
            (i, i + step) for i in range(n_dp)
            if 0 <= i + step and i // SPAN == (i + step) // SPAN
        ]
        return lax.ppermute(block, ALL, route)

    def swap(block):
        return lax.ppermute(block, "core", [(0, 1), (1, 0)])

    weights = lax.all_gather(flat_params, ALL, axis=0, tiled=True)

    row = lambda v: v.reshape(1, n)
    here, *outbound = call(
        send_kernel, "send", 63,
        [shape((n // 2, width + 128), BF16)] + [shape((cap, width + 128), BF16)] * 4,
        [row(edge_owner), row(edge_src), row(edge_dst), row(edge_rot), node_feats],
        numbers=me.reshape(1),
    )
    arrived = [shift(r, s) for r, s in zip(outbound, STEPS)]

    tab = rot_table.transpose(1, 0, 2).reshape(K * n_rot, K)
    tabt = rot_table.transpose(2, 0, 1).reshape(K * n_rot, K)

    def rotate(rows_in, name, cost=None):
        slots = sum(r.shape[0] for r in rows_in)
        return call(
            lambda *refs: rotate_kernel(len(rows_in), *refs), name, 63,
            [
                shape((2 * slots, width), BF16), shape((slots, n), BF16),
                shape((slots, n_rot), BF16),
            ],
            [*rows_in, tab, node_grad],
            [
                pltpu.VMEM((slots // 8, 240, 256), BF16), pltpu.VMEM((30, slots, 256), F32),
                pltpu.VMEM((32, slots, 256), F32), pltpu.VMEM((30, slots, 256), F32),
            ],
            cost=cost,
        )

    both_a, hot_a, turn_a = rotate([here] + arrived[:2], "rotate_first")
    both_a_other = swap(both_a)
    last, both_a = lax.optimization_barrier((arrived[2:], both_a))
    both_b, hot_b, turn_b = rotate(
        last, "rotate_last",
        pl.CostEstimate(flops=10**10, bytes_accessed=10**8, transcendentals=0),
    )
    both_b_other = swap(both_b)
    both, hots, turns = [both_a, both_b], [hot_a, hot_b], [turn_a, turn_b]

    n_send, n_keep = n_z // 2 * (2 * n_x - 1), n_z // 2
    blocks = call(
        lambda *refs: grad_kernel(n_z, n_x, *refs), "weight_terms", 63,
        [shape((rows, 128), BF16)] * n_send + [shape((rows, 128), F32)] * n_keep,
        both + [both_a_other, both_b_other],
        [pltpu.VMEM((rows * n_dp, 128), F32)],
        numbers=me.reshape(1),
    )
    turns, blocks = lax.optimization_barrier((turns, list(blocks)))
    mats = call(
        back_kernel, "back", 63,
        [shape((t.shape[0] // 8, 240, 256), BF16) for t in turns],
        [tabt] + turns,
        [pltpu.VMEM((30, t.shape[0], 256), F32) for t in turns],
    )
    kept = blocks[n_send:]
    kept[0], mats = lax.optimization_barrier((kept[0], mats))
    sums, moves = {}, iter(blocks)
    for at, r in enumerate(reversed(range(0, n_z, 2))):
        total = kept[at]
        for b, o in square(n_x):
            route = [
                (i * n_x + j, (i ^ b) * n_x + (j + o) % n_x)
                for i in range(n_z) for j in range(n_x)
            ]
            total = total + lax.ppermute(next(moves), ("z", "x"), route).astype(F32)
        sums[r] = total
    for bit in [1 << i for i in range(1, n_z.bit_length() - 1)]:
        for r in reversed(range(bit, n_z, 2 * bit)):
            last_term = sums[r].astype(BF16)
            got = lax.ppermute(last_term, "z", [(s, s ^ bit) for s in range(n_z)])
            if 2 * bit < n_z:
                sums[r ^ bit] = sums[r ^ bit] + got.astype(F32)
    weights, _ = lax.optimization_barrier((weights, last_term))
    slots = n // 2 + 4 * cap
    (node_out,) = call(
        message_kernel, "messages", 63,
        [shape((n, width), BF16)],
        [weights, *both, *mats, *hots],
        [
            pltpu.VMEM((rows * n_dp, 128), F32), pltpu.VMEM((32, slots, 128), F32),
            pltpu.VMEM((30, slots, 128), F32), pltpu.VMEM((slots, width), BF16),
        ],
    )
    got, node_out = lax.optimization_barrier((got, node_out))
    result = sums[0] + got.astype(F32)
    weight_grad = result * (1.0 / math.sqrt(n * n_dp))
    return (node_out, weight_grad)


def chips(mesh):
    n_dp = mesh.shape["dp"]
    line = list(mesh.devices.reshape(-1, n_dp)[0])
    coords = [getattr(d, "coords", None) for d in line]
    n_x = 2 if coords[0] is None else len({c[0] for c in coords})
    return n_dp // (2 * n_x), n_x


def solution(mesh):
    n_z, n_x = chips(mesh)
    fine = Mesh(
        np.asarray(mesh.devices).reshape(mesh.shape["groups"], n_z, n_x, 2),
        ("groups", "z", "x", "core"),
    )
    every = ("groups",) + ALL
    placed = (
        P(every, None),
        P(every, None),
        P(ALL, None),
        P(),
        P(every),
        P(every),
        P(every),
        P(every, None),
    )
    return jax.shard_map(
        lambda *args: on_device(n_z, n_x, *args),
        mesh=fine,
        in_specs=placed,
        out_specs=(P(every, None), P(every, None)),
        check_vma=False,
    )
```

```python
import math

import jax
import jax.numpy as jnp
import numpy as np
from jax import lax
from jax.experimental import pallas as pl
from jax.experimental.pallas import tpu as pltpu
from jax.sharding import Mesh, PartitionSpec as P

K = 29
SPAN = 8
STEPS = (-2, 2, -1, 1)
F32 = jnp.float32
BF16 = jnp.bfloat16
ALL = ("z", "x", "core")


def dot(a, b):
    return jnp.dot(a, b, preferred_element_type=F32)


def iota(shape, dim):
    return lax.broadcasted_iota(jnp.int32, shape, dim)


def hot(cond):
    return jnp.where(cond, 1.0, 0.0).astype(BF16)


def column(row):
    n = row.shape[1]
    eye = iota((n, n), 0) == iota((n, n), 1)
    return jnp.sum(jnp.where(eye, row.astype(F32), 0.0), axis=1, keepdims=True)


def dp_index(n_x):
    return (lax.axis_index("z") * n_x + lax.axis_index("x")) * 2 + lax.axis_index("core")


def send_kernel(me_ref, owner_ref, src_ref, dst_ref, rot_ref, feats_ref, *outs):
    n = feats_ref.shape[0]
    width = feats_ref.shape[1]
    half, cap = n // 2, n // 4
    off_row = (owner_ref[...] - me_ref[0]).astype(F32)
    off = column(off_row)
    before = (off == off_row) & (iota((n, n), 0) < iota((n, n), 1))
    slot = jnp.sum(jnp.where(before, 1.0, 0.0), axis=0, keepdims=True)
    for q, step in enumerate(STEPS):
        slot = jnp.where(off_row == step, slot + float(half + q * cap), slot)
    slots = half + 4 * cap
    here = slot == iota((slots, n), 0).astype(F32)

    def pick(row):
        return jnp.sum(jnp.where(here, row, 0.0), axis=1, keepdims=True)

    source = pick(src_ref[...].astype(F32) + 1.0) - 1.0
    target = pick(dst_ref[...].astype(F32) + 1.0)
    turns = pick(rot_ref[...].astype(F32))
    source_hot = hot(source == iota((slots, n), 1).astype(F32))
    lane = iota((slots, 128), 1)
    ids = jnp.where(lane == 0, target, jnp.where(lane == 1, turns, 0.0)).astype(BF16)
    spans = [(0, half)] + [(half + q * cap, cap) for q in range(4)]
    for o, (at, size) in zip(outs, spans):
        o[:, width:] = ids[at : at + size]
    for j, w in chunks():
        cols = slice(j * 128, (j + w) * 128)
        rows = dot(source_hot, feats_ref[:, cols]).astype(BF16)
        for o, (at, size) in zip(outs, spans):
            o[:, cols] = rows[at : at + size]


def turn(mats_ref, src_ref, res_ref):
    lanes = src_ref.shape[2]
    for g in range(src_ref.shape[1] // 8):
        rhs = src_ref[:, 8 * g : 8 * g + 8, :].reshape(256, lanes).astype(BF16)
        res = dot(mats_ref[g], rhs)
        res_ref[:, 8 * g : 8 * g + 8, :] = res.reshape(30, 8, lanes)


def build(table_ref, rot_hot, mats_ref, tmp_ref):
    n = rot_hot.shape[0]
    n_rot = rot_hot.shape[1]
    spread = hot(iota((K, 256), 1) // 8 == iota((K, 256), 0))
    wide = dot(table_ref[...], spread).astype(BF16)
    own = (iota((n, 256), 1) % 8) == (iota((n, 256), 0) % 8)
    for k in range(K):
        tmp_ref[k] = jnp.where(own, dot(rot_hot, wide[k * n_rot : (k + 1) * n_rot]), 0.0)
    tmp_ref[K] = jnp.zeros((n, 256), F32)
    for g in range(n // 8):
        mats_ref[g] = tmp_ref[:, 8 * g : 8 * g + 8, :].reshape(240, 256).astype(BF16)


def chunks():
    j = 0
    while j < K:
        w = min(4, K - j)
        yield j, w
        j += w


def joined(refs, cols):
    return jnp.concatenate([r[:, cols] for r in refs], axis=0)


def number(ids, lane):
    at = iota(ids.shape, 1) == lane
    return jnp.sum(jnp.where(at, ids.astype(F32), 0.0), axis=1, keepdims=True)


def rotate_kernel(count, *refs):
    raw, (tab_ref, grad_ref) = refs[:count], refs[count : count + 2]
    both_ref, hot_ref, turn_ref, mats_ref, tmp_ref, in_ref, res_ref = refs[count + 2 :]
    n = grad_ref.shape[0]
    n_rot = tab_ref.shape[0] // K
    width = grad_ref.shape[1]
    ids = joined(raw, slice(width, width + 128))
    slots = ids.shape[0]
    target_hot = hot(number(ids, 0) - 1.0 == iota((slots, n), 1).astype(F32))
    rot_hot = hot(number(ids, 1) == iota((slots, n_rot), 1).astype(F32))
    hot_ref[...] = target_hot
    turn_ref[...] = rot_hot
    for j, w in chunks():
        cols = slice(j * 128, (j + w) * 128)
        rows = joined(raw, cols).astype(F32)
        back = dot(target_hot, grad_ref[:, cols])
        for i in range(w):
            in_ref[j + i, :, :128] = rows[:, 128 * i : 128 * i + 128]
            in_ref[j + i, :, 128:] = back[:, 128 * i : 128 * i + 128]
    for j in range(K, 32):
        in_ref[j] = jnp.zeros((slots, 256), F32)
    build(tab_ref, rot_hot, mats_ref, tmp_ref)
    turn(mats_ref, in_ref, res_ref)
    for k in range(K):
        cols = slice(k * 128, (k + 1) * 128)
        both_ref[:slots, cols] = res_ref[k, :, :128].astype(BF16)
        both_ref[slots:, cols] = res_ref[k, :, 128:].astype(BF16)


def back_kernel(tabt_ref, *refs):
    for i in range(2):
        build(tabt_ref, refs[i][...], refs[2 + i], refs[4 + i])


def products(parts, flat, low, high):

    def left(first, i, end):
        at = slice((first + i) * 128, (first + end) * 128)
        return [p[: p.shape[0] // 2, at] for p in parts]

    def right(first, width):
        at = slice(first * 128, (first + width) * 128)
        return [p[p.shape[0] // 2 :, at] for p in parts]

    def emit(base, width, firsts, rhs):
        unit = width * 128
        i, end = max(0, (low - base) // unit), min(width, -(-(high - base) // unit))
        if i >= end:
            return
        lhs = jnp.concatenate([v for f in firsts for v in left(f, i, end)], axis=0)
        res = lax.dot_general(
            lhs, jnp.concatenate(rhs(), axis=0), (((0,), (0,)), ((), ())),
            preferred_element_type=F32,
        )
        for b in range(width):
            at = pl.ds(base + i * unit + b, (end - i) * 128, stride=width)
            flat[at, :] = res[:, b * 128 : (b + 1) * 128]

    emit(0, 7, (0,), lambda: right(0, 7))
    base = 49 * 128
    for first, width in ((7, 6), (19, 5)):
        mid = first + width
        emit(base, width, (first, mid), lambda: right(first, width) + right(mid, width))
        base += width * width * 128
        emit(
            base, width, (first, mid),
            lambda: right(mid, width) + [-v for v in right(first, width)],
        )
        base += width * width * 128


def owner_row(n_x, me, r, o, rows):
    chip, core = me // 2, me % 2
    z, x = chip // n_x, chip % n_x
    start = (((z ^ r) * n_x + (x + o) % n_x) * 2 + core) * rows
    return pl.multiple_of(start, 8) if rows % 8 == 0 else start


def first_kernel(n_z, n_x, me_ref, *refs):
    parts, out_ref, flat = refs[:4], refs[4], refs[5]
    rows = out_ref.shape[0]
    start = owner_row(n_x, me_ref[0], n_z - 1, 1, rows)
    for chip in range(n_z * n_x):

        @pl.when(start // (2 * rows) == chip)
        def _():
            products(parts, flat, chip * 2 * rows, (chip + 1) * 2 * rows)

    out_ref[...] = flat[pl.ds(start, rows), :].astype(BF16)


def grad_kernel(n_z, n_x, me_ref, *refs):
    parts, outs, flat = refs[:4], refs[4:-1], refs[-1]
    products(parts, flat, 0, flat.shape[0])
    rows = outs[0].shape[0]
    order = [(r, o) for o in list(range(1, n_x)) + [0] for r in reversed(range(n_z))]
    for ref, (r, o) in zip(outs, order[1:]):
        start = owner_row(n_x, me_ref[0], r, o, rows)
        ref[...] = flat[pl.ds(start, rows), :].astype(ref.dtype)


def message_kernel(w_ref, *refs):
    both, mats, hots = refs[0:2], refs[2:4], refs[4:6]
    out_ref, flat, in_ref, res_ref, wide_ref = refs[6:]
    n = out_ref.shape[0]
    slots = in_ref.shape[1]
    part = w_ref.shape[0] // 16
    for p in range(16):
        flat[p * part : (p + 1) * part, :] = w_ref[p * part : (p + 1) * part, :].astype(F32)

    def h(first, end):
        return jnp.concatenate(
            [r[: r.shape[0] // 2, first * 128 : end * 128] for r in both], axis=0
        )

    def fill(j, wide):
        for i in range(wide.shape[1] // 128):
            in_ref[j + i] = wide[:, 128 * i : 128 * i + 128]

    def weight(base, width, b, many):
        parts = [
            flat[pl.ds(base + b + t, width * 128, stride=width), :].astype(BF16)
            for t in range(many)
        ]
        return parts[0] if many == 1 else jnp.concatenate(parts, axis=1)

    def rounded(v):
        return v.astype(BF16).astype(F32)

    def pairs(width):
        return [(b, min(2, width - b)) for b in range(0, width, 2)]

    h0 = h(0, 7)
    for b, many in pairs(7):
        fill(b, rounded(dot(h0, weight(0, 7, b, many))))
    base = 49 * 128
    for first, width in ((7, 6), (19, 5)):
        mid, end = first + width, first + 2 * width
        pair = jnp.concatenate([h(first, mid), h(mid, end)], axis=0)
        for b, many in pairs(width):
            real = dot(pair, weight(base, width, b, many))
            imag = dot(pair, weight(base + width * width * 128, width, b, many))
            fill(first + b, rounded(real[:slots] - imag[slots:]))
            fill(mid + b, rounded(imag[:slots] + real[slots:]))
        base += 2 * width * width * 128
    for j in range(K, 32):
        in_ref[j] = jnp.zeros((slots, 128), F32)
    at = 0
    for m in mats:
        size = m.shape[0] * 8
        turn(m, in_ref.at[:, at : at + size, :], res_ref.at[:, at : at + size, :])
        at += size
    for k in range(K):
        wide_ref[:, k * 128 : (k + 1) * 128] = res_ref[k].astype(BF16)
    target = jnp.concatenate([r[...] for r in hots], axis=0).astype(F32).T.astype(BF16)
    for j, w in chunks():
        cols = slice(j * 128, (j + w) * 128)
        out_ref[:, cols] = dot(target, wide_ref[:, cols]).astype(BF16)


def shape(dims, kind):
    return jax.ShapeDtypeStruct(dims, kind)


def whole(like):
    zeros = (0,) * len(like.shape)
    return pl.BlockSpec(like.shape, lambda i: zeros, pipeline_mode=pl.Buffered(1))


def call(kernel, name, mib, outs, operands, scratch=(), numbers=None, cost=None):
    first = [] if numbers is None else [pl.BlockSpec(memory_space=pltpu.SMEM)]
    return pl.pallas_call(
        kernel,
        grid=(1,),
        out_shape=outs,
        in_specs=first + [whole(v) for v in operands],
        out_specs=[whole(o) for o in outs],
        scratch_shapes=list(scratch),
        compiler_params=pltpu.CompilerParams(vmem_limit_bytes=mib * 1024 * 1024),
        cost_estimate=cost,
        name=name,
    )(*(() if numbers is None else (numbers,)), *operands)


def on_device(
    n_z, n_x, node_feats, node_grad, flat_params, rot_table, edge_src, edge_dst, edge_rot,
    edge_owner,
):
    n = edge_src.shape[0]
    cap = n // 4
    width = node_feats.shape[1]
    rows = flat_params.shape[0]
    n_dp = n_z * n_x * 2
    n_rot = rot_table.shape[0]
    me = dp_index(n_x)
    smem = pl.BlockSpec(memory_space=pltpu.SMEM)

    def shift(block, step):
        route = [
            (i, i + step) for i in range(n_dp)
            if 0 <= i + step and i // SPAN == (i + step) // SPAN
        ]
        return lax.ppermute(block, ALL, route)

    def swap(block):
        return lax.ppermute(block, "core", [(0, 1), (1, 0)])

    weights = lax.all_gather(flat_params, ALL, axis=0, tiled=True)

    row = lambda v: v.reshape(1, n)
    here, *outbound = call(
        send_kernel, "send", 62,
        [shape((n // 2, width + 128), BF16)] + [shape((cap, width + 128), BF16)] * 4,
        [row(edge_owner), row(edge_src), row(edge_dst), row(edge_rot), node_feats],
        numbers=me.reshape(1),
    )
    arrived = [shift(r, s) for r, s in zip(outbound, STEPS)]

    tab = rot_table.transpose(1, 0, 2).reshape(K * n_rot, K)
    tabt = rot_table.transpose(2, 0, 1).reshape(K * n_rot, K)

    def rotate(rows_in, name, cost=None):
        slots = sum(r.shape[0] for r in rows_in)
        return call(
            lambda *refs: rotate_kernel(len(rows_in), *refs), name, 62,
            [
                shape((2 * slots, width), BF16), shape((slots, n), BF16),
                shape((slots, n_rot), BF16),
            ],
            [*rows_in, tab, node_grad],
            [
                pltpu.VMEM((slots // 8, 240, 256), BF16), pltpu.VMEM((30, slots, 256), F32),
                pltpu.VMEM((32, slots, 256), F32), pltpu.VMEM((30, slots, 256), F32),
            ],
            cost=cost,
        )

    both_a, hot_a, turn_a = rotate([here] + arrived[:2], "rotate_first")
    both_a_other = swap(both_a)
    last, both_a = lax.optimization_barrier((arrived[2:], both_a))
    both_b, hot_b, turn_b = rotate(
        last, "rotate_last",
        pl.CostEstimate(flops=10**10, bytes_accessed=10**8, transcendentals=0),
    )
    both_b_other = swap(both_b)
    both, hots, turns = [both_a, both_b], [hot_a, hot_b], [turn_a, turn_b]

    n_send = n_z * (n_x - 1)
    terms = both + [both_a_other, both_b_other]
    (first_block,) = call(
        lambda *refs: first_kernel(n_z, n_x, *refs), "first_terms", 63,
        [shape((rows, 128), BF16)], terms, [pltpu.VMEM((rows * n_dp, 128), F32)],
        numbers=me.reshape(1),
    )
    terms, first_block = lax.optimization_barrier((terms, first_block))
    others = call(
        lambda *refs: grad_kernel(n_z, n_x, *refs), "weight_terms", 63,
        [shape((rows, 128), BF16)] * (n_send - 1) + [shape((rows, 128), F32)] * n_z,
        terms, [pltpu.VMEM((rows * n_dp, 128), F32)],
        numbers=me.reshape(1),
    )
    turns, others = lax.optimization_barrier((turns, list(others)))
    mats = call(
        back_kernel, "back", 62,
        [shape((t.shape[0] // 8, 240, 256), BF16) for t in turns],
        [tabt] + turns,
        [pltpu.VMEM((30, t.shape[0], 256), F32) for t in turns],
    )
    blocks = [first_block] + others
    kept = blocks[n_send:]
    kept[1], mats = lax.optimization_barrier((kept[1], mats))
    sums = {}
    for at, r in enumerate(reversed(range(n_z))):
        total = kept[at]
        for o in range(1, n_x):
            got = lax.ppermute(
                blocks[(o - 1) * n_z + at], "x", [(s, (s + o) % n_x) for s in range(n_x)]
            )
            total = total + got.astype(F32)
        sums[r] = total
    for bit in [1 << i for i in range(n_z.bit_length() - 1)]:
        for r in reversed(range(bit, n_z, 2 * bit)):
            term = sums[r].astype(BF16)
            if (bit, r) == (1, 1):
                last_term = term
            got = lax.ppermute(term, "z", [(s, s ^ bit) for s in range(n_z)])
            if 2 * bit < n_z:
                sums[r ^ bit] = sums[r ^ bit] + got.astype(F32)
    weights, _ = lax.optimization_barrier((weights, last_term))
    slots = n // 2 + 4 * cap
    (node_out,) = call(
        message_kernel, "messages", 62,
        [shape((n, width), BF16)],
        [weights, *both, *mats, *hots],
        [
            pltpu.VMEM((rows * n_dp, 128), F32), pltpu.VMEM((32, slots, 128), F32),
            pltpu.VMEM((30, slots, 128), F32), pltpu.VMEM((slots, width), BF16),
        ],
    )
    got, node_out = lax.optimization_barrier((got, node_out))
    result = sums[0] + got.astype(F32)
    weight_grad = result * (1.0 / math.sqrt(n * n_dp))
    return (node_out, weight_grad)


def chips(mesh):
    n_dp = mesh.shape["dp"]
    line = list(mesh.devices.reshape(-1, n_dp)[0])
    coords = [getattr(d, "coords", None) for d in line]
    n_x = 2 if coords[0] is None else len({c[0] for c in coords})
    return n_dp // (2 * n_x), n_x


def solution(mesh):
    n_z, n_x = chips(mesh)
    fine = Mesh(
        np.asarray(mesh.devices).reshape(mesh.shape["groups"], n_z, n_x, 2),
        ("groups", "z", "x", "core"),
    )
    every = ("groups",) + ALL
    placed = (
        P(every, None),
        P(every, None),
        P(ALL, None),
        P(),
        P(every),
        P(every),
        P(every),
        P(every, None),
    )
    return jax.shard_map(
        lambda *args: on_device(n_z, n_x, *args),
        mesh=fine,
        in_specs=placed,
        out_specs=(P(every, None), P(every, None)),
        check_vma=False,
    )
```

```python
import math

import jax
import jax.numpy as jnp
import numpy as np
from jax import lax
from jax.experimental import pallas as pl
from jax.experimental.pallas import tpu as pltpu
from jax.sharding import Mesh, PartitionSpec as P

K = 29
SPAN = 8
STEPS = (-2, 2, -1, 1)
F32 = jnp.float32
BF16 = jnp.bfloat16
ALL = ("z", "x", "core")


def dot(a, b):
    return jnp.dot(a, b, preferred_element_type=F32)


def iota(shape, dim):
    return lax.broadcasted_iota(jnp.int32, shape, dim)


def hot(cond):
    return jnp.where(cond, 1.0, 0.0).astype(BF16)


def column(row):
    n = row.shape[1]
    eye = iota((n, n), 0) == iota((n, n), 1)
    return jnp.sum(jnp.where(eye, row.astype(F32), 0.0), axis=1, keepdims=True)


def dp_index(n_x):
    return (lax.axis_index("z") * n_x + lax.axis_index("x")) * 2 + lax.axis_index("core")


def send_kernel(me_ref, owner_ref, src_ref, dst_ref, rot_ref, feats_ref, *outs):
    n = feats_ref.shape[0]
    width = feats_ref.shape[1]
    half, cap = n // 2, n // 4
    off_row = (owner_ref[...] - me_ref[0]).astype(F32)
    off = column(off_row)
    before = (off == off_row) & (iota((n, n), 0) < iota((n, n), 1))
    slot = jnp.sum(jnp.where(before, 1.0, 0.0), axis=0, keepdims=True)
    for q, step in enumerate(STEPS):
        slot = jnp.where(off_row == step, slot + float(half + q * cap), slot)
    slots = half + 4 * cap
    here = slot == iota((slots, n), 0).astype(F32)

    def pick(row):
        return jnp.sum(jnp.where(here, row, 0.0), axis=1, keepdims=True)

    source = pick(src_ref[...].astype(F32) + 1.0) - 1.0
    target = pick(dst_ref[...].astype(F32) + 1.0)
    turns = pick(rot_ref[...].astype(F32))
    source_hot = hot(source == iota((slots, n), 1).astype(F32))
    lane = iota((slots, 128), 1)
    ids = jnp.where(lane == 0, target, jnp.where(lane == 1, turns, 0.0)).astype(BF16)
    spans = [(0, half)] + [(half + q * cap, cap) for q in range(4)]
    for o, (at, size) in zip(outs, spans):
        o[:, width:] = ids[at : at + size]
    for j, w in chunks():
        cols = slice(j * 128, (j + w) * 128)
        rows = dot(source_hot, feats_ref[:, cols]).astype(BF16)
        for o, (at, size) in zip(outs, spans):
            o[:, cols] = rows[at : at + size]


def turn(mats_ref, src_ref, res_ref):
    lanes = src_ref.shape[2]
    for g in range(src_ref.shape[1] // 8):
        rhs = src_ref[:, 8 * g : 8 * g + 8, :].reshape(256, lanes).astype(BF16)
        res = dot(mats_ref[g], rhs)
        res_ref[:, 8 * g : 8 * g + 8, :] = res.reshape(30, 8, lanes)


def build(table_ref, rot_hot, mats_ref, tmp_ref):
    n = rot_hot.shape[0]
    n_rot = rot_hot.shape[1]
    spread = hot(iota((K, 256), 1) // 8 == iota((K, 256), 0))
    wide = dot(table_ref[...], spread).astype(BF16)
    own = (iota((n, 256), 1) % 8) == (iota((n, 256), 0) % 8)
    for k in range(K):
        tmp_ref[k] = jnp.where(own, dot(rot_hot, wide[k * n_rot : (k + 1) * n_rot]), 0.0)
    tmp_ref[K] = jnp.zeros((n, 256), F32)
    for g in range(n // 8):
        mats_ref[g] = tmp_ref[:, 8 * g : 8 * g + 8, :].reshape(240, 256).astype(BF16)


def chunks():
    j = 0
    while j < K:
        w = min(4, K - j)
        yield j, w
        j += w


def joined(refs, cols):
    return jnp.concatenate([r[:, cols] for r in refs], axis=0)


def number(ids, lane):
    at = iota(ids.shape, 1) == lane
    return jnp.sum(jnp.where(at, ids.astype(F32), 0.0), axis=1, keepdims=True)


def rotate_kernel(count, *refs):
    raw, (tab_ref, grad_ref) = refs[:count], refs[count : count + 2]
    both_ref, hot_ref, turn_ref, mats_ref, tmp_ref, in_ref, res_ref = refs[count + 2 :]
    n = grad_ref.shape[0]
    n_rot = tab_ref.shape[0] // K
    width = grad_ref.shape[1]
    ids = joined(raw, slice(width, width + 128))
    slots = ids.shape[0]
    target_hot = hot(number(ids, 0) - 1.0 == iota((slots, n), 1).astype(F32))
    rot_hot = hot(number(ids, 1) == iota((slots, n_rot), 1).astype(F32))
    hot_ref[...] = target_hot
    turn_ref[...] = rot_hot
    for j, w in chunks():
        cols = slice(j * 128, (j + w) * 128)
        rows = joined(raw, cols).astype(F32)
        back = dot(target_hot, grad_ref[:, cols])
        for i in range(w):
            in_ref[j + i, :, :128] = rows[:, 128 * i : 128 * i + 128]
            in_ref[j + i, :, 128:] = back[:, 128 * i : 128 * i + 128]
    for j in range(K, 32):
        in_ref[j] = jnp.zeros((slots, 256), F32)
    build(tab_ref, rot_hot, mats_ref, tmp_ref)
    turn(mats_ref, in_ref, res_ref)
    for k in range(K):
        cols = slice(k * 128, (k + 1) * 128)
        both_ref[:slots, cols] = res_ref[k, :, :128].astype(BF16)
        both_ref[slots:, cols] = res_ref[k, :, 128:].astype(BF16)


def back_kernel(tabt_ref, *refs):
    for i in range(2):
        build(tabt_ref, refs[i][...], refs[2 + i], refs[4 + i])


def leaving(n_z):
    return sorted(range(n_z), key=lambda r: (r % 2 == 0, -r))


def grad_kernel(n_z, n_x, me_ref, *refs):
    parts, outs, flat = refs[:4], refs[4:-1], refs[-1]
    chip, core = me_ref[0] // 2, me_ref[0] % 2
    z, x = chip // n_x, chip % n_x

    def left(first, width):
        at = slice(first * 128, (first + width) * 128)
        return [p[: p.shape[0] // 2, at] for p in parts]

    def right(first, width):
        at = slice(first * 128, (first + width) * 128)
        return [p[p.shape[0] // 2 :, at] for p in parts]

    def outer(lhs, rhs):
        return lax.dot_general(lhs, rhs, (((0,), (0,)), ((), ())), preferred_element_type=F32)

    def emit(base, width, res):
        for b in range(width):
            flat[pl.ds(base + b, width * 128, stride=width), :] = res[:, b * 128 : (b + 1) * 128]

    emit(0, 7, outer(jnp.concatenate(left(0, 7), axis=0), jnp.concatenate(right(0, 7), axis=0)))
    base = 49 * 128
    for first, width in ((7, 6), (19, 5)):
        lhs = jnp.concatenate(left(first, width) + left(first + width, width), axis=0)
        real, imag = right(first, width), right(first + width, width)
        emit(base, width, outer(lhs, jnp.concatenate(real + imag, axis=0)))
        base += width * width * 128
        emit(base, width, outer(lhs, jnp.concatenate(imag + [-v for v in real], axis=0)))
        base += width * width * 128

    rows = outs[0].shape[0]
    at_out = 0
    for o in list(range(1, n_x)) + [0]:
        for r in leaving(n_z):
            start = (((z ^ r) * n_x + (x + o) % n_x) * 2 + core) * rows
            if rows % 8 == 0:
                start = pl.multiple_of(start, 8)
            ref = outs[at_out]
            ref[...] = flat[pl.ds(start, rows), :].astype(ref.dtype)
            at_out += 1


def message_kernel(w_ref, *refs):
    both, mats, hots = refs[0:2], refs[2:4], refs[4:6]
    out_ref, flat, in_ref, res_ref, wide_ref = refs[6:]
    n = out_ref.shape[0]
    slots = in_ref.shape[1]
    part = w_ref.shape[0] // 16
    for p in range(16):
        flat[p * part : (p + 1) * part, :] = w_ref[p * part : (p + 1) * part, :].astype(F32)

    def h(first, end):
        return jnp.concatenate(
            [r[: r.shape[0] // 2, first * 128 : end * 128] for r in both], axis=0
        )

    def fill(j, wide):
        for i in range(wide.shape[1] // 128):
            in_ref[j + i] = wide[:, 128 * i : 128 * i + 128]

    def weight(base, width, b, many):
        parts = [
            flat[pl.ds(base + b + t, width * 128, stride=width), :].astype(BF16)
            for t in range(many)
        ]
        return parts[0] if many == 1 else jnp.concatenate(parts, axis=1)

    def rounded(v):
        return v.astype(BF16).astype(F32)

    def pairs(width):
        return [(b, min(2, width - b)) for b in range(0, width, 2)]

    h0 = h(0, 7)
    for b, many in pairs(7):
        fill(b, rounded(dot(h0, weight(0, 7, b, many))))
    base = 49 * 128
    for first, width in ((7, 6), (19, 5)):
        mid, end = first + width, first + 2 * width
        pair = jnp.concatenate([h(first, mid), h(mid, end)], axis=0)
        for b, many in pairs(width):
            real = dot(pair, weight(base, width, b, many))
            imag = dot(pair, weight(base + width * width * 128, width, b, many))
            fill(first + b, rounded(real[:slots] - imag[slots:]))
            fill(mid + b, rounded(imag[:slots] + real[slots:]))
        base += 2 * width * width * 128
    for j in range(K, 32):
        in_ref[j] = jnp.zeros((slots, 128), F32)
    at = 0
    for m in mats:
        size = m.shape[0] * 8
        turn(m, in_ref.at[:, at : at + size, :], res_ref.at[:, at : at + size, :])
        at += size
    for k in range(K):
        wide_ref[:, k * 128 : (k + 1) * 128] = res_ref[k].astype(BF16)
    target = jnp.concatenate([r[...] for r in hots], axis=0).astype(F32).T.astype(BF16)
    for j, w in chunks():
        cols = slice(j * 128, (j + w) * 128)
        out_ref[:, cols] = dot(target, wide_ref[:, cols]).astype(BF16)


def shape(dims, kind):
    return jax.ShapeDtypeStruct(dims, kind)


def whole(like):
    zeros = (0,) * len(like.shape)
    return pl.BlockSpec(like.shape, lambda i: zeros, pipeline_mode=pl.Buffered(1))


def call(kernel, name, mib, outs, operands, scratch=(), numbers=None, cost=None):
    first = [] if numbers is None else [pl.BlockSpec(memory_space=pltpu.SMEM)]
    return pl.pallas_call(
        kernel,
        grid=(1,),
        out_shape=outs,
        in_specs=first + [whole(v) for v in operands],
        out_specs=[whole(o) for o in outs],
        scratch_shapes=list(scratch),
        compiler_params=pltpu.CompilerParams(vmem_limit_bytes=mib * 1024 * 1024),
        cost_estimate=cost,
        name=name,
    )(*(() if numbers is None else (numbers,)), *operands)


def on_device(
    n_z, n_x, node_feats, node_grad, flat_params, rot_table, edge_src, edge_dst, edge_rot,
    edge_owner,
):
    n = edge_src.shape[0]
    cap = n // 4
    width = node_feats.shape[1]
    rows = flat_params.shape[0]
    n_dp = n_z * n_x * 2
    n_rot = rot_table.shape[0]
    me = dp_index(n_x)
    smem = pl.BlockSpec(memory_space=pltpu.SMEM)

    def shift(block, step):
        route = [
            (i, i + step) for i in range(n_dp)
            if 0 <= i + step and i // SPAN == (i + step) // SPAN
        ]
        return lax.ppermute(block, ALL, route)

    def swap(block):
        return lax.ppermute(block, "core", [(0, 1), (1, 0)])

    weights = lax.all_gather(flat_params, ALL, axis=0, tiled=True)

    row = lambda v: v.reshape(1, n)
    here, *outbound = call(
        send_kernel, "send", 62,
        [shape((n // 2, width + 128), BF16)] + [shape((cap, width + 128), BF16)] * 4,
        [row(edge_owner), row(edge_src), row(edge_dst), row(edge_rot), node_feats],
        numbers=me.reshape(1),
    )
    arrived = [shift(r, s) for r, s in zip(outbound, STEPS)]

    tab = rot_table.transpose(1, 0, 2).reshape(K * n_rot, K)
    tabt = rot_table.transpose(2, 0, 1).reshape(K * n_rot, K)

    def rotate(rows_in, name, cost=None):
        slots = sum(r.shape[0] for r in rows_in)
        return call(
            lambda *refs: rotate_kernel(len(rows_in), *refs), name, 62,
            [
                shape((2 * slots, width), BF16), shape((slots, n), BF16),
                shape((slots, n_rot), BF16),
            ],
            [*rows_in, tab, node_grad],
            [
                pltpu.VMEM((slots // 8, 240, 256), BF16), pltpu.VMEM((30, slots, 256), F32),
                pltpu.VMEM((32, slots, 256), F32), pltpu.VMEM((30, slots, 256), F32),
            ],
            cost=cost,
        )

    both_a, hot_a, turn_a = rotate([here] + arrived[:2], "rotate_first")
    both_a_other = swap(both_a)
    last, both_a = lax.optimization_barrier((arrived[2:], both_a))
    both_b, hot_b, turn_b = rotate(
        last, "rotate_last",
        pl.CostEstimate(flops=10**10, bytes_accessed=10**8, transcendentals=0),
    )
    both_b_other = swap(both_b)
    both, hots, turns = [both_a, both_b], [hot_a, hot_b], [turn_a, turn_b]

    n_send = n_z * (n_x - 1)
    blocks = call(
        lambda *refs: grad_kernel(n_z, n_x, *refs), "weight_terms", 63,
        [shape((rows, 128), BF16)] * (n_send + n_z),
        both + [both_a_other, both_b_other],
        [pltpu.VMEM((rows * n_dp, 128), F32)],
        numbers=me.reshape(1),
    )
    turns, blocks = lax.optimization_barrier((turns, list(blocks)))
    mats = call(
        back_kernel, "back", 62,
        [shape((t.shape[0] // 8, 240, 256), BF16) for t in turns],
        [tabt] + turns,
        [pltpu.VMEM((30, t.shape[0], 256), F32) for t in turns],
    )
    kept = blocks[n_send:]
    kept[0], mats = lax.optimization_barrier((kept[0], mats))
    sums = {}
    for at, r in enumerate(leaving(n_z)):
        total = kept[at].astype(F32)
        for o in range(1, n_x):
            got = lax.ppermute(
                blocks[(o - 1) * n_z + at], "x", [(s, (s + o) % n_x) for s in range(n_x)]
            )
            total = total + got.astype(F32)
        sums[r] = total
    for bit in [1 << i for i in range(n_z.bit_length() - 1)]:
        for r in reversed(range(bit, n_z, 2 * bit)):
            last_term = sums[r].astype(BF16)
            got = lax.ppermute(last_term, "z", [(s, s ^ bit) for s in range(n_z)])
            if 2 * bit < n_z:
                sums[r ^ bit] = sums[r ^ bit] + got.astype(F32)
    weights, _ = lax.optimization_barrier((weights, last_term))
    slots = n // 2 + 4 * cap
    (node_out,) = call(
        message_kernel, "messages", 62,
        [shape((n, width), BF16)],
        [weights, *both, *mats, *hots],
        [
            pltpu.VMEM((rows * n_dp, 128), F32), pltpu.VMEM((32, slots, 128), F32),
            pltpu.VMEM((30, slots, 128), F32), pltpu.VMEM((slots, width), BF16),
        ],
    )
    got, node_out = lax.optimization_barrier((got, node_out))
    result = sums[0] + got.astype(F32)
    weight_grad = result * (1.0 / math.sqrt(n * n_dp))
    return (node_out, weight_grad)


def chips(mesh):
    n_dp = mesh.shape["dp"]
    line = list(mesh.devices.reshape(-1, n_dp)[0])
    coords = [getattr(d, "coords", None) for d in line]
    n_x = 2 if coords[0] is None else len({c[0] for c in coords})
    return n_dp // (2 * n_x), n_x


def solution(mesh):
    n_z, n_x = chips(mesh)
    fine = Mesh(
        np.asarray(mesh.devices).reshape(mesh.shape["groups"], n_z, n_x, 2),
        ("groups", "z", "x", "core"),
    )
    every = ("groups",) + ALL
    placed = (
        P(every, None),
        P(every, None),
        P(ALL, None),
        P(),
        P(every),
        P(every),
        P(every),
        P(every, None),
    )
    return jax.shard_map(
        lambda *args: on_device(n_z, n_x, *args),
        mesh=fine,
        in_specs=placed,
        out_specs=(P(every, None), P(every, None)),
        check_vma=False,
    )
```
